512 devices in a mesh: row: 16 (over z_lo, core), col: 32 (over x, z_hi, y).
Axes of the slice: x: 4, y: 4, z: 16 (z_hi: 2, z_lo: 8; z = z_hi * 8 + z_lo), core: 2. Of those that a mesh axis runs over, the one named last changes fastest.
Arguments:
- pair: bfloat16 [256, 256, 128], P('row', 'col'), may hold values from -6 to 6
- pair_mask: int32 [256, 256], P('row', 'col'), may hold values 0 or 1
- contact_mask: int32 [256, 256], P('row', 'col'), may hold values 0 or 1
- dilations: int32 [2], replicated, may hold values from 1 to 8, as said below
- w_proj: bfloat16 [128, 512], replicated, may hold values from -0.5 to 0.5
- w_gate: bfloat16 [128, 128], replicated, may hold values from -0.5 to 0.5
- w_out: bfloat16 [128, 128], replicated, may hold values from -0.5 to 0.5
- conv_one: bfloat16 [9, 128, 128], replicated, may hold values from -0.1875 to 0.1875
- conv_two: bfloat16 [9, 128, 128], replicated, may hold values from -0.1875 to 0.1875
- cotangent: bfloat16 [256, 256, 128], P('row', 'col'), may hold values from -6 to 6
Outputs:
- output: bfloat16 [256, 256, 128], P('row', 'col')
- grad_pair: bfloat16 [256, 256, 128], P('row', 'col')
- grad_one: float32 [9, 128, 128], replicated
- grad_two: float32 [9, 128, 128], replicated
The draws below stay inside these ranges and needn't reach their ends.
Inputs may be any that keep to these rules, and one draw needn't show every extreme that they name: `dilations`: one of the two rates equals 8, the other is smaller.
All inputs are finite; a program needn't handle non-finite values. No bound on the sum of `pair_mask` or of `contact_mask` on one device may be relied on, other than what follows from the above.
Results may differ from the reference program's by a relative error of at most 0.015.
Values may be sent and summed in bfloat16 or wider, within the bound.
A program may use at most 64 MiB of HBM per device.

```python
import jax
import jax.numpy as jnp
from jax import lax

C = 128
H = 128
DMAX = 8
N = 256


def draw_dilations(key, part):
    key = jax.random.fold_in(key, 7)
    other = jax.random.randint(jax.random.fold_in(key, 11), (), 1, DMAX)
    which = jax.random.randint(jax.random.fold_in(key, 12), (), 0, 2)
    return jnp.where(jnp.arange(2) == which, DMAX, other).astype(jnp.int32)


def place_ends(entries, stream_key, smallest, high):
    extent = entries.shape
    spot = [jax.random.randint(jax.random.fold_in(stream_key, axis), (), 0, extent[axis]) for axis in range(len(extent))]
    entries = entries.at[tuple(spot)].set(smallest)
    longest = extent.index(max(extent))
    spot[longest] = (spot[longest] + 1) % extent[longest]
    return entries.at[tuple(spot)].set(high)


def shard_levels(stream_key, dims, cuts, low, largest):
    def one(axis_at, parts):
        steps = jax.random.uniform(jax.random.fold_in(jax.random.fold_in(stream_key, 6), axis_at), (parts,), jnp.float32, low / len(cuts), largest / len(cuts))
        return jnp.repeat(jnp.exp(steps), dims[axis_at] // parts).reshape((-1,) + (1,) * (len(dims) - axis_at - 1))

    gain = one(*cuts[0])
    for cut in cuts[1:]:
        gain = gain * one(*cut)
    return gain


def gaussian(rng, shape, deviation, most, pieces=(), dtype=jnp.bfloat16):
    array = deviation * jax.random.normal(rng, shape, jnp.float32)
    if pieces:
        array = array * shard_levels(rng, shape, pieces, -0.22, 0.18)
    return jnp.clip(array, -most, most).astype(dtype)


def setup_inputs(seed: int = 0) -> dict:
    key_list = jax.random.split(jax.random.key(seed), 11)
    return {
        "pair": gaussian(key_list[0], (N, N, C), 1.0, 6.0, ((0, 16), (1, 32))),
        "pair_mask": place_ends((jax.random.randint(key_list[1], (N, N), 0, 4) < 3).astype(jnp.int32), jax.random.fold_in(key_list[1], 1), 0, 1),
        "contact_mask": place_ends((jax.random.randint(key_list[2], (N, N), 0, 2) < 1).astype(jnp.int32), jax.random.fold_in(key_list[2], 1), 0, 1),
        "dilations": draw_dilations(jax.random.fold_in(key_list[10], 71), 0),
        "w_proj": gaussian(key_list[4], (C, 4 * H), C ** -0.5, 0.5),
        "w_gate": gaussian(key_list[5], (C, C), C ** -0.5, 0.5),
        "w_out": gaussian(key_list[6], (H, C), H ** -0.5, 0.5),
        "conv_one": gaussian(key_list[7], (9, C, C), (9 * C) ** -0.5, 0.1875),
        "conv_two": gaussian(key_list[8], (9, C, C), (9 * C) ** -0.5, 0.1875),
        "cotangent": gaussian(key_list[9], (N, N, C), 1.0, 6.0, ((0, 16), (1, 32))),
    }


EPSILON = 1e-05

def layer_norm(values):
    centre = values - lax.optimization_barrier(jnp.mean(values, axis=-1, keepdims=True))
    spread = lax.optimization_barrier(jnp.mean(centre * centre, axis=-1, keepdims=True))
    return centre * lax.rsqrt(spread + EPSILON)

def pad_border(field):
    return jnp.pad(field, ((DMAX, DMAX), (DMAX, DMAX), (0, 0)))

def window(padded, dilation, row_tap, col_tap, height, breadth):
    row_start = (DMAX + (row_tap - 1) * dilation).astype(jnp.int32)
    col_start = (DMAX + (col_tap - 1) * dilation).astype(jnp.int32)
    return lax.dynamic_slice(padded, (row_start, col_start, jnp.int32(0)), (height, breadth, padded.shape[2]))

def conv_forward(field, weights, dilation):
    height, breadth, channels = field.shape
    padded = pad_border(field)
    result = jnp.zeros((height * breadth, weights.shape[2]), jnp.float32)
    for tap_index in range(9):
        shifted = window(padded, dilation, tap_index // 3, tap_index % 3, height, breadth)
        result = result + jnp.dot(shifted.reshape(-1, channels), weights[tap_index], preferred_element_type=jnp.float32)
    return result

def conv_transpose(field, weights, dilation):
    height, breadth, channels = field.shape
    padded = pad_border(field)
    result = jnp.zeros((height * breadth, weights.shape[1]), jnp.float32)
    for tap_index in range(9):
        shifted = window(padded, dilation, 2 - tap_index // 3, 2 - tap_index % 3, height, breadth)
        result = result + jnp.dot(shifted.reshape(-1, channels), weights[tap_index].T, preferred_element_type=jnp.float32)
    return result

def weight_grad(field, upstream, dilation):
    height, breadth, channels = field.shape
    padded = pad_border(field)
    upstream_flat = upstream.reshape(height * breadth, -1)
    grads = []
    for tap_index in range(9):
        shifted = window(padded, dilation, tap_index // 3, tap_index % 3, height, breadth)
        grads.append(lax.dot_general(shifted.reshape(-1, channels), upstream_flat, (((0,), (0,)), ((), ())), preferred_element_type=jnp.float32))
    return jnp.stack(grads, axis=0)

def reference(pair, pair_mask, contact_mask, dilations, w_proj, w_gate, w_out, conv_one, conv_two, cotangent):
    total, _, channels = pair.shape
    hidden = w_out.shape[0]
    pair_flat = pair.astype(jnp.float32).reshape(-1, channels)
    normed = layer_norm(pair_flat).astype(jnp.bfloat16)
    projected = jnp.dot(normed, w_proj, preferred_element_type=jnp.float32)
    mask_col = pair_mask.reshape(-1, 1).astype(jnp.float32)
    left_side = (mask_col * jax.nn.sigmoid(projected[:, hidden:2 * hidden]) * projected[:, :hidden]).astype(jnp.bfloat16)
    right_side = (mask_col * jax.nn.sigmoid(projected[:, 3 * hidden:]) * projected[:, 2 * hidden:3 * hidden]).astype(jnp.bfloat16)
    left_full = left_side.reshape(total, total, hidden).astype(jnp.float32)
    right_full = right_side.reshape(total, total, hidden).astype(jnp.float32)
    products = jnp.einsum('ikh,jkh->ijh', left_full, right_full)
    product_norm = layer_norm(products.reshape(-1, hidden)).astype(jnp.bfloat16)
    gating = jax.nn.sigmoid(jnp.dot(normed, w_gate, preferred_element_type=jnp.float32))
    updated = (pair_flat + gating * jnp.dot(product_norm, w_out, preferred_element_type=jnp.float32)).astype(jnp.bfloat16)
    updated_f = updated.astype(jnp.float32)
    centre = updated_f - lax.optimization_barrier(jnp.mean(updated_f, axis=-1, keepdims=True))
    inv_spread = lax.rsqrt(lax.optimization_barrier(jnp.mean(centre * centre, axis=-1, keepdims=True)) + EPSILON)
    scaled = centre * inv_spread
    contact = contact_mask.reshape(-1, 1).astype(jnp.float32)
    first_in = (scaled * contact).astype(jnp.bfloat16).reshape(total, total, channels)
    first_pre = conv_forward(first_in, conv_one, dilations[0])
    sigma = jax.nn.sigmoid(first_pre)
    second_in = (first_pre * sigma).astype(jnp.bfloat16).reshape(total, total, channels)
    second_pre = conv_forward(second_in, conv_two, dilations[1])
    output = (updated_f + second_pre).astype(jnp.bfloat16).reshape(total, total, channels)
    grad_two = weight_grad(second_in, cotangent, dilations[1]) / total
    grad_hidden = conv_transpose(cotangent, conv_two, dilations[1])
    grad_pre = (grad_hidden * sigma * (1.0 + first_pre * (1.0 - sigma))).astype(jnp.bfloat16).reshape(total, total, channels)
    grad_one = weight_grad(first_in, grad_pre, dilations[0]) / total
    grad_input = conv_transpose(grad_pre, conv_one, dilations[0]) * contact
    grad_norm = inv_spread * (grad_input - lax.optimization_barrier(jnp.mean(grad_input, axis=-1, keepdims=True)) - scaled * lax.optimization_barrier(jnp.mean(grad_input * scaled, axis=-1, keepdims=True)))
    grad_pair = (cotangent.astype(jnp.float32).reshape(-1, channels) + grad_norm).astype(jnp.bfloat16).reshape(total, total, channels)
    return (output, grad_pair, grad_one, grad_two)
```

```python
import functools

import jax
import jax.numpy as jnp
from jax import lax
from jax.experimental import pallas as pl
from jax.experimental.pallas import tpu as pltpu
from jax.sharding import PartitionSpec as P

EPSILON = 1e-05
MESH = pl.DeviceIdType.MESH
BF = jnp.bfloat16
F32 = jnp.float32
ROWS = 16
COLS = 32


def signal(sem, row, col):
    pl.semaphore_signal(sem, inc=1, device_id=(row, col), device_id_type=MESH)


def remote(src, dst, send_sem, recv_sem, row, col):
    return pltpu.make_async_remote_copy(
        src_ref=src,
        dst_ref=dst,
        send_sem=send_sem,
        recv_sem=recv_sem,
        device_id=(row, col),
        device_id_type=MESH,
    )


def wait_bytes(ref, sem):
    pltpu.make_async_copy(ref, ref, sem).wait()


def each(low, high, body):
    def step(k, carry):
        body(k)
        return carry

    lax.fori_loop(low, high, step, 0)


def plane_peer(col, k):
    x = lax.rem(col // 8 + k // 4, 4)
    y = lax.rem(lax.rem(col, 4) + lax.rem(k, 4), 4)
    return x * 8 + lax.rem(col // 4, 2) * 4 + y


def plane_slot(col):
    return (col // 8) * 4 + lax.rem(col, 4)


def layer_norm(values):
    centre = values - jnp.mean(values, axis=-1, keepdims=True)
    spread = jnp.mean(centre * centre, axis=-1, keepdims=True)
    return centre * lax.rsqrt(spread + EPSILON)


def mask_column(mask, height, breadth):
    pixels = height * breadth
    pix = lax.broadcasted_iota(jnp.int32, (pixels, height), 0) // breadth
    pick = (pix == lax.broadcasted_iota(jnp.int32, (pixels, height), 1)).astype(F32)
    spread = jnp.dot(pick, mask.astype(F32), preferred_element_type=F32)
    place = lax.rem(lax.broadcasted_iota(jnp.int32, (pixels, breadth), 0), breadth)
    lane = lax.broadcasted_iota(jnp.int32, (pixels, breadth), 1)
    return jnp.sum(jnp.where(place == lane, spread, 0.0), axis=1, keepdims=True)


def triangle_kernel(
    pair_ref, pmask_ref, cmask_ref, wproj_ref, wgate_ref, wout_ref, cot_ref,
    updated_ref, first_ref, cots_ref,
    left, right, halves, first, cots, sums,
    l_send, l_recv, l_far, r_send0, r_recv0, r_send, r_recv, r_relay,
    c_send, c_recv, c_send2, c_recv2, f_send, f_recv, f_send2, f_recv2,
):
    row = lax.axis_index("row")
    col = lax.axis_index("col")
    far = (col // 8) * 8 + (1 - lax.rem(col // 4, 2)) * 4 + lax.rem(col, 4)
    sibling = row + 1 - 2 * lax.rem(row, 2)
    turn_row = col // 2
    up = lax.rem(row + ROWS - 1, ROWS)
    down = lax.rem(row + 1, ROWS)
    barrier = pltpu.get_barrier_semaphore()
    each(1, 16, lambda k: signal(barrier, row, plane_peer(col, k)))
    each(1, 8, lambda k: signal(barrier, lax.rem(row + 2 * k, ROWS), col))
    signal(barrier, row, far)
    signal(barrier, sibling, col)
    for shift in (1, 2):
        signal(barrier, row, lax.rem(col + shift, COLS))
        signal(barrier, row, lax.rem(col + COLS - shift, COLS))
    signal(barrier, up, col)
    signal(barrier, down, col)
    for half in range(2):
        @pl.when((turn_row != row) | (2 * row + half != col))
        def _():
            signal(barrier, turn_row, 2 * row + half)

    pair = pair_ref[...].astype(F32)
    normed = layer_norm(pair).astype(BF)
    projected = jnp.dot(normed, wproj_ref[...], preferred_element_type=F32)
    mask = mask_column(pmask_ref[...], 16, 8)
    left[col] = (mask * jax.nn.sigmoid(projected[:, 128:256]) * projected[:, :128]).astype(BF)
    halves[...] = (
        (mask * jax.nn.sigmoid(projected[:, 384:]) * projected[:, 256:384])
        .astype(BF)
        .reshape(2, 64, 128)
    )
    cots[7] = cot_ref[...]

    diagonal = turn_row == row

    @pl.when(diagonal)
    def _():
        pl.semaphore_wait(barrier, 31)

    @pl.when(jnp.logical_not(diagonal))
    def _():
        pl.semaphore_wait(barrier, 32)

    for half in range(2):
        there = 2 * row + half

        @pl.when((turn_row != row) | (there != col))
        def _():
            remote(
                halves.at[half], right.at[col], r_send0.at[half],
                r_recv0.at[lax.rem(col, 2)], turn_row, there,
            ).start()

        @pl.when((turn_row == row) & (there == col))
        def _():
            right[col] = halves[half]

    mine = left.at[col]
    remote(mine, mine, l_send, l_far, row, far).start()
    each(1, 16, lambda k: remote(mine, mine, l_send, l_recv, row, plane_peer(col, k)).start())

    for half in range(2):
        there = 2 * row + half

        @pl.when((turn_row != row) | (there != col))
        def _():
            wait_bytes(halves.at[half], r_send0.at[half])
            wait_bytes(right.at[0], r_recv0.at[half])

    two = right.at[pl.ds(2 * row, 2)]
    each(1, 8, lambda k: remote(
        two, two, r_send, r_relay.at[row // 2], lax.rem(row + 2 * k, ROWS), col).start())
    remote(two, two, r_send, r_recv, sibling, col).start()

    far_block = left.at[far]
    wait_bytes(far_block, l_far)
    each(1, 16, lambda k: remote(
        far_block, far_block, l_send, l_recv, row, plane_peer(col, k)).start())

    def along_cols(buf, send_sem, recv_sem):
        for n, shift in enumerate((1, 2, -1, -2)):
            remote(
                buf.at[7], buf.at[7 - shift], send_sem.at[n], recv_sem.at[n],
                row, lax.rem(col + COLS + shift, COLS),
            ).start()

    def wait_cols(buf, send_sem, recv_sem):
        for n in range(4):
            wait_bytes(buf.at[7], send_sem.at[n])
            wait_bytes(buf.at[7], recv_sem.at[n])

    def along_rows(buf, send_sem, recv_sem):
        band = buf.at[pl.ds(5, 5)]
        remote(band, buf.at[pl.ds(0, 5)], send_sem.at[0], recv_sem.at[0], down, col).start()
        remote(band, buf.at[pl.ds(10, 5)], send_sem.at[1], recv_sem.at[1], up, col).start()

    def wait_rows(buf, send_sem, recv_sem):
        for n in range(2):
            wait_bytes(buf.at[pl.ds(5, 5)], send_sem.at[n])
            wait_bytes(buf.at[pl.ds(0, 5)], recv_sem.at[n])

    along_cols(cots, c_send, c_recv)

    def relay(k):
        p = lax.rem(row + ROWS - 2 * k, ROWS)
        block = right.at[pl.ds(2 * p, 2)]
        wait_bytes(block, r_relay.at[p // 2])
        remote(block, block, r_send, r_recv, sibling, col).start()

    each(1, 8, relay)
    gating = jax.nn.sigmoid(jnp.dot(normed, wgate_ref[...], preferred_element_type=F32))
    wait_cols(cots, c_send, c_recv)
    along_rows(cots, c_send2, c_recv2)

    wait_bytes(right.at[pl.ds(0, 16)], r_recv)
    wait_bytes(left.at[pl.ds(0, 30)], l_recv)

    for part in range(4):
        def add(c, total):
            a = left[c, pl.ds(part * 32, 32), :].astype(F32).reshape(4, 1, 8, 128)
            b = right[c].astype(F32).reshape(1, 8, 8, 128)
            return total + a * b

        total = lax.fori_loop(0, COLS, add, jnp.zeros((4, 8, 8, 128), F32))
        sums[pl.ds(part * 32, 32), :] = jnp.sum(total, axis=2).reshape(32, 128)

    product_norm = layer_norm(sums[...]).astype(BF)
    updated = (
        pair + gating * jnp.dot(product_norm, wout_ref[...], preferred_element_type=F32)
    ).astype(BF)
    updated_ref[...] = updated
    contact = mask_column(cmask_ref[...], 16, 8)
    first[7] = (layer_norm(updated.astype(F32)) * contact).astype(BF)
    along_cols(first, f_send, f_recv)
    wait_rows(cots, c_send2, c_recv2)
    cots_ref[...] = cots[...]
    wait_cols(first, f_send, f_recv)
    along_rows(first, f_send2, f_recv2)
    wait_bytes(right.at[pl.ds(0, 30)], r_send)
    wait_bytes(left.at[pl.ds(0, 31)], l_send)
    wait_rows(first, f_send2, f_recv2)
    first_ref[...] = first[...]


def conv_kernel(
    rates_ref, updated_ref, cmask_ref, first_ref, cots_ref, one_ref, two_ref,
    output_ref, gpair_ref, grads_ref,
    field, taps, cfield, ctaps, hidden, htaps, gpre, gtaps,
):
    row = lax.axis_index("row")
    col = lax.axis_index("col")
    one_rate = rates_ref[0]
    two_rate = rates_ref[1]

    to = lax.broadcasted_iota(jnp.int32, (128, 128), 0)
    at = lax.broadcasted_iota(jnp.int32, (128, 128), 1)
    flip = ((lax.rem(to, 16) * 8 + to // 16) == at).astype(BF)
    flip_back = ((lax.rem(to, 8) * 16 + to // 8) == at).astype(BF)

    def unfold(src, dst):
        for n in range(15):
            dr, dc = n // 5 - 1, n % 5 - 2
            inside = (row + dr >= 0) & (row + dr < ROWS) & (col + dc >= 0) & (col + dc < COLS)
            cell = jnp.dot(flip, src[n], preferred_element_type=F32)
            dst[pl.ds((dc + 2) * 8, 8), pl.ds((dr + 1) * 16, 16), :] = jnp.where(
                inside, cell, 0.0
            ).reshape(8, 16, 128)

    def shifted(src, dst, start, rate, length, sign):
        for r in range(3):
            wide = src.shape[1]
            move = lax.rem(2 * wide - (start + sign * (r - 1) * rate), wide)
            dst[r] = pltpu.roll(src[...], move, 1)[:, :length].astype(BF)

    def windows(src, start, rate, count, sign, rows=None):
        found = []
        for t in range(9):
            at = pl.ds(start + sign * (t % 3 - 1) * rate, count)
            piece = src[t // 3, at] if rows is None else src[t // 3, at, rows, :]
            found.append(piece.reshape(-1, 128))
        return jnp.concatenate(found, axis=1)

    unfold(first_ref, field)
    unfold(cots_ref, cfield)
    shifted(field, taps, 8, one_rate, 32, 1)
    shifted(cfield, ctaps, 8, two_rate, 32, -1)

    weights_one = one_ref[...].reshape(1152, 128)
    weights_two = two_ref[...].reshape(1152, 128)
    back_two = jnp.concatenate([two_ref[t].T for t in range(9)], axis=0)
    back_one = jnp.concatenate([one_ref[t].T for t in range(9)], axis=0)

    pre = jnp.dot(windows(taps, 8, one_rate, 24, 1), weights_one, preferred_element_type=F32)
    grad_hidden = jnp.dot(
        windows(ctaps, 8, two_rate, 24, -1), back_two, preferred_element_type=F32
    )
    c_at = lax.broadcasted_iota(jnp.int32, (24, 32, 128), 0) + (col * 8 - 8)
    r_at = lax.broadcasted_iota(jnp.int32, (24, 32, 128), 1) + (row * 16 - 8)
    inside = (c_at >= 0) & (c_at < 256) & (r_at >= 0) & (r_at < 256)
    sigma = jax.nn.sigmoid(pre)
    hidden[...] = jnp.where(inside, (pre * sigma).reshape(24, 32, 128), 0.0)
    gpre[...] = jnp.where(
        inside, (grad_hidden * sigma * (1.0 + pre * (1.0 - sigma))).reshape(24, 32, 128), 0.0
    )
    shifted(hidden, htaps, 8, two_rate, 16, 1)
    shifted(gpre, gtaps, 8, one_rate, 16, -1)
    cot_own = cfield[pl.ds(16, 8), pl.ds(16, 16), :].reshape(128, 128)
    gpre_own = gpre[pl.ds(8, 8), pl.ds(8, 16), :].reshape(128, 128).astype(BF)
    second_taps = windows(htaps, 8, two_rate, 8, 1)
    first_taps = windows(taps, 16, one_rate, 8, 1, pl.ds(8, 16))
    over = (((0,), (0,)), ((), ()))
    grads_ref[pl.ds(1152, 1152), :] = lax.dot_general(
        second_taps, cot_own.astype(BF), over, preferred_element_type=F32
    ).astype(BF)
    grads_ref[pl.ds(0, 1152), :] = lax.dot_general(
        first_taps, gpre_own, over, preferred_element_type=F32
    ).astype(BF)
    def back(value):
        return jnp.dot(flip_back, value, preferred_element_type=F32).astype(BF)

    second_pre = jnp.dot(back(second_taps), weights_two, preferred_element_type=F32)
    grad_in = jnp.dot(
        back(windows(gtaps, 8, one_rate, 8, -1)), back_one, preferred_element_type=F32
    )
    updated = updated_ref[...].astype(F32)
    output_ref[...] = (updated + second_pre).astype(BF)
    contact = mask_column(cmask_ref[...], 16, 8)
    grad_in = grad_in * contact
    centre = updated - jnp.mean(updated, axis=-1, keepdims=True)
    inv = lax.rsqrt(jnp.mean(centre * centre, axis=-1, keepdims=True) + EPSILON)
    scaled = centre * inv
    grad_norm = inv * (
        grad_in
        - jnp.mean(grad_in, axis=-1, keepdims=True)
        - scaled * jnp.mean(grad_in * scaled, axis=-1, keepdims=True)
    )
    gpair_ref[...] = (cots_ref[7].astype(F32) + grad_norm).astype(BF)


def reduce_kernel(
    grads_ref, out_ref, parts, own, pieces, final,
    send1, recv1, send2, recv2, send3, recv3, send4, recv4,
):
    row = lax.axis_index("row")
    col = lax.axis_index("col")
    me = plane_slot(col)
    place = row * 2 + lax.rem(col // 4, 2)
    base = (col // 8) * 8 + lax.rem(col, 4)

    def line(q):
        return q // 2, base + lax.rem(q, 2) * 4

    barrier = pltpu.get_barrier_semaphore()
    each(1, 16, lambda k: signal(barrier, row, plane_peer(col, k)))
    each(1, 32, lambda k: signal(barrier, *line(lax.rem(place + k, 32))))
    pl.semaphore_wait(barrier, 46)

    def scatter(k):
        peer = plane_peer(col, k)
        remote(grads_ref.at[plane_slot(peer)], parts.at[me], send1, recv1, row, peer).start()

    each(1, 16, scatter)
    parts[me] = grads_ref[me]
    most = parts.at[pl.ds(0, 15)]
    wait_bytes(most, recv1)
    total = parts[0].astype(F32)
    for n in range(1, 16):
        total = total + parts[n].astype(F32)
    own[...] = total.astype(BF).reshape(9, 16, 128)

    for j in range(9):
        @pl.when(place != 3 * j)
        def _():
            remote(own.at[j], pieces.at[place], send2, recv2, *line(3 * j)).start()

    owner = (lax.rem(place, 3) == 0) & (place < 27)
    piece = place // 3

    @pl.when(owner)
    def _():
        pieces[place] = own[piece]
        wait_bytes(own.at[pl.ds(0, 8)], send2)
        wait_bytes(pieces.at[pl.ds(0, 31)], recv2)
        total = pieces[0].astype(F32)
        for n in range(1, 32):
            total = total + pieces[n].astype(F32)
        final[me, piece] = total.astype(BF)
        block = final.at[me, piece]
        each(1, 32, lambda k: remote(
            block, block, send3, recv3, *line(lax.rem(place + k, 32))).start())
        wait_bytes(own.at[pl.ds(0, 8)], recv3)

    @pl.when(jnp.logical_not(owner))
    def _():
        wait_bytes(own, send2)
        wait_bytes(own, recv3)

    whole = final.at[me]
    each(1, 16, lambda k: remote(whole, whole, send4, recv4, row, plane_peer(col, k)).start())
    wait_bytes(most, send1)

    @pl.when(owner)
    def _():
        wait_bytes(pieces.at[pl.ds(0, 31)], send3)

    wait_bytes(final.at[pl.ds(0, 15)], recv4)
    wait_bytes(final.at[pl.ds(0, 15)], send4)
    out_ref[...] = final[...].reshape(16, 144, 128)


VMEM = pltpu.VMEM
DMA = pltpu.SemaphoreType.DMA


def whole(count):
    return [pl.BlockSpec(memory_space=pltpu.VMEM)] * count


def shape(dims, dtype):
    return jax.ShapeDtypeStruct(dims, dtype)


def local(
    pair, pair_mask, contact_mask, dilations, w_proj, w_gate, w_out, conv_one, conv_two, cotangent
):
    pair = pair.reshape(128, 128)
    cot = cotangent.reshape(128, 128)
    updated, first, cots = pl.pallas_call(
        triangle_kernel,
        out_shape=(shape((128, 128), BF), shape((15, 128, 128), BF), shape((15, 128, 128), BF)),
        in_specs=whole(7),
        out_specs=tuple(whole(3)),
        scratch_shapes=[
            VMEM((32, 128, 128), BF), VMEM((32, 64, 128), BF), VMEM((2, 64, 128), BF),
            VMEM((15, 128, 128), BF), VMEM((15, 128, 128), BF), VMEM((128, 128), F32),
            DMA, DMA, DMA, DMA((2,)), DMA((2,)), DMA, DMA, DMA((8,)),
            DMA((4,)), DMA((4,)), DMA((2,)), DMA((2,)),
            DMA((4,)), DMA((4,)), DMA((2,)), DMA((2,)),
        ],
        compiler_params=pltpu.CompilerParams(
            collective_id=1, has_side_effects=True, vmem_limit_bytes=40 << 20
        ),
    )(pair, pair_mask, contact_mask, w_proj, w_gate, w_out, cot)
    output, grad_pair, grads = pl.pallas_call(
        conv_kernel,
        out_shape=(shape((128, 128), BF), shape((128, 128), BF), shape((2304, 128), BF)),
        in_specs=[pl.BlockSpec(memory_space=pltpu.SMEM)] + whole(6),
        out_specs=tuple(whole(3)),
        scratch_shapes=[
            VMEM((40, 48, 128), F32), VMEM((3, 40, 32, 128), BF),
            VMEM((40, 48, 128), F32), VMEM((3, 40, 32, 128), BF),
            VMEM((24, 32, 128), F32), VMEM((3, 24, 16, 128), BF),
            VMEM((24, 32, 128), F32), VMEM((3, 24, 16, 128), BF),
        ],
        compiler_params=pltpu.CompilerParams(vmem_limit_bytes=40 << 20),
    )(dilations, updated, contact_mask, first, cots, conv_one, conv_two)
    total = pl.pallas_call(
        reduce_kernel,
        out_shape=shape((16, 144, 128), BF),
        in_specs=whole(1),
        out_specs=whole(1)[0],
        scratch_shapes=[
            VMEM((16, 144, 128), BF), VMEM((9, 16, 128), BF), VMEM((32, 16, 128), BF),
            VMEM((16, 9, 16, 128), BF), DMA, DMA, DMA, DMA, DMA, DMA, DMA, DMA,
        ],
        compiler_params=pltpu.CompilerParams(
            collective_id=2, has_side_effects=True, vmem_limit_bytes=40 << 20
        ),
    )(grads.reshape(16, 144, 128))
    total = total.reshape(2, 9, 128, 128).astype(F32) * (1.0 / 256.0)
    return (output.reshape(16, 8, 128), grad_pair.reshape(16, 8, 128), total[0], total[1])


def solution(mesh):
    in_specs = (
        P("row", "col", None), P("row", "col"), P("row", "col"), P(), P(), P(), P(), P(), P(),
        P("row", "col", None),
    )
    out_specs = (P("row", "col", None), P("row", "col", None), P(), P())
    return jax.shard_map(local, mesh=mesh, in_specs=in_specs, out_specs=out_specs, check_vma=False)
```

```python
import jax
import jax.numpy as jnp
from jax import lax
from jax.experimental import pallas as pl
from jax.experimental.pallas import tpu as pltpu
from jax.sharding import PartitionSpec as P

EPSILON = 1e-05
MESH = pl.DeviceIdType.MESH
BF = jnp.bfloat16
F32 = jnp.float32
ROWS = 16
COLS = 32
SHIFTS = (1, 2, -1, -2)


def signal(sem, row, col):
    pl.semaphore_signal(sem, inc=1, device_id=(row, col), device_id_type=MESH)


def remote(src, dst, send_sem, recv_sem, row, col):
    return pltpu.make_async_remote_copy(
        src_ref=src,
        dst_ref=dst,
        send_sem=send_sem,
        recv_sem=recv_sem,
        device_id=(row, col),
        device_id_type=MESH,
    )


def wait_bytes(ref, sem):
    pltpu.make_async_copy(ref, ref, sem).wait()


def each(low, high, body):
    def step(k, carry):
        body(k)
        return carry

    lax.fori_loop(low, high, step, 0)


def plane_peer(col, k):
    x = lax.rem(col // 8 + k // 4, 4)
    y = lax.rem(lax.rem(col, 4) + lax.rem(k, 4), 4)
    return x * 8 + lax.rem(col // 4, 2) * 4 + y


def plane_slot(col):
    return (col // 8) * 4 + lax.rem(col, 4)


def on_map(col):
    return (col >= 0) & (col < COLS)


def layer_norm(values):
    centre = values - jnp.mean(values, axis=-1, keepdims=True)
    spread = jnp.mean(centre * centre, axis=-1, keepdims=True)
    return centre * lax.rsqrt(spread + EPSILON)


def mask_column(mask):
    pix = lax.broadcasted_iota(jnp.int32, (128, 8), 0)
    lane = lax.broadcasted_iota(jnp.int32, (128, 8), 1)
    pick = (lax.rem(pix, 8) == lane).astype(F32)
    spread = jnp.dot(pick, mask.astype(F32), preferred_element_type=F32)
    place = lax.broadcasted_iota(jnp.int32, (128, 16), 0) // 8
    at = lax.broadcasted_iota(jnp.int32, (128, 16), 1)
    return jnp.sum(jnp.where(place == at, spread, 0.0), axis=1, keepdims=True)


def shifted(src, dst, start, rate, length, sign):
    wide = src.shape[1]
    for r in range(3):
        move = lax.rem(2 * wide - (start + sign * (r - 1) * rate), wide)
        dst[r] = pltpu.roll(src[...], move, 1)[:, :length].astype(BF)


def windows(src, start, rate, count, sign, rows=None):
    found = []
    for t in range(9):
        at = pl.ds(start + sign * (t % 3 - 1) * rate, count)
        piece = src[t // 3, at] if rows is None else src[t // 3, at, rows, :]
        found.append(piece.reshape(-1, 128))
    return jnp.concatenate(found, axis=1)


def kernel(
    pair_h, pmask_h, cmask_h, rates_h, wproj_h, wgate_h, wout_h, one_h, two_h, cot_h,
    output_ref, gpair_ref, total_ref,
    pair_v, pmask_v, cmask_v, rates_s, wproj_v, wgate_v, wout_v, one_v, two_v, in_sem,
    left, right, halves, first, cots, sums,
    field, taps, cfield, ctaps, hidden, htaps, gpre, gtaps, ghid,
    grads, parts, own, pieces, final,
    l_send, l_recv, l_far, r_send0, r_recv0, r_send, r_recv, r_relay,
    c_send, c_recv, c_send2, c_recv2, f_send, f_recv, f_send2, f_recv2,
    send1, recv1, send2, recv2, send3, recv3, send4, recv4,
):
    row = lax.axis_index("row")
    col = lax.axis_index("col")
    far = (col // 8) * 8 + (1 - lax.rem(col // 4, 2)) * 4 + lax.rem(col, 4)
    sibling = row + 1 - 2 * lax.rem(row, 2)
    turn_row = col // 2
    turn_col = 4 * lax.rem(row, 8)
    me = plane_slot(col)
    place = row * 2 + lax.rem(col // 4, 2)
    base = (col // 8) * 8 + lax.rem(col, 4)

    def line(q):
        return q // 2, base + lax.rem(q, 2) * 4

    with jax.named_scope("start"):
        loads = [
            pltpu.make_async_copy(src, dst, in_sem.at[n])
            for n, (src, dst) in enumerate((
                (pair_h, pair_v), (pmask_h, pmask_v), (wproj_h, wproj_v), (cot_h, cots.at[7]),
                (wgate_h, wgate_v), (wout_h, wout_v), (cmask_h, cmask_v), (rates_h, rates_s),
                (two_h, two_v), (one_h, one_v),
            ))
        ]
        for load in loads:
            load.start()
        barrier = pltpu.get_barrier_semaphore()
        each(1, 16, lambda k: signal(barrier, row, plane_peer(col, k)))
        each(1, 32, lambda k: signal(barrier, *line(lax.rem(place + k, 32))))
        for shift in (1, 2, -1, -2):
            @pl.when(on_map(col + shift))
            def _():
                signal(barrier, row, col + shift)
        for n in range(4):
            @pl.when((turn_row != row) | (turn_col + n != col))
            def _():
                signal(barrier, turn_row, turn_col + n)

    with jax.named_scope("project"):
        for n in (0, 1, 2):
            loads[n].wait()
        pair = pair_v[...].astype(F32)
        normed = layer_norm(pair).astype(BF)
        projected = jnp.dot(normed, wproj_v[...], preferred_element_type=F32)
        mask = mask_column(pmask_v[...])
        left[col] = (mask * jax.nn.sigmoid(projected[:, 128:256]) * projected[:, :128]).astype(BF)
        halves[...] = (
            (mask * jax.nn.sigmoid(projected[:, 384:]) * projected[:, 256:384])
            .astype(BF)
            .reshape(2, 64, 128)
        )
        loads[3].wait()

    with jax.named_scope("barrier"):
        fixed = (turn_row == row) & (lax.rem(row, 8) == col // 4)
        pl.semaphore_wait(
            barrier,
            50 - jnp.where(fixed, 1, 0) + jnp.minimum(col, 2) + jnp.minimum(COLS - 1 - col, 2),
        )

    with jax.named_scope("turn"):
        def turn(half, low):
            return low * 8 + col // 4, 2 * row + half

        for half in range(2):
            for low in range(2):
                t_row, t_col = turn(half, low)

                @pl.when((t_row != row) | (t_col != col))
                def _():
                    remote(
                        halves.at[half], right.at[col], r_send0.at[2 * half + low],
                        r_recv0.at[lax.rem(col, 4)], t_row, t_col,
                    ).start()

                @pl.when((t_row == row) & (t_col == col))
                def _():
                    right[col] = halves[half]

        mine = left.at[col]
        remote(mine, mine, l_send, l_far, row, far).start()
        each(1, 16, lambda k: remote(mine, mine, l_send, l_recv, row, plane_peer(col, k)).start())

        for half in range(2):
            for low in range(2):
                t_row, t_col = turn(half, low)

                @pl.when((t_row != row) | (t_col != col))
                def _():
                    wait_bytes(halves.at[half], r_send0.at[2 * half + low])
        for n in range(4):
            @pl.when((turn_row != row) | (turn_col + n != col))
            def _():
                wait_bytes(right.at[0], r_recv0.at[n])

    with jax.named_scope("spread"):
        four = right.at[pl.ds(turn_col, 4)]
        each(1, 4, lambda k: remote(
            four, four, r_send, r_relay.at[lax.rem(row, 8) // 2],
            (row // 8) * 8 + lax.rem(row + 2 * k, 8), col).start())
        remote(four, four, r_send, r_recv, sibling, col).start()

    with jax.named_scope("farwait"):
        far_block = left.at[far]
        wait_bytes(far_block, l_far)
        each(1, 16, lambda k: remote(
            far_block, far_block, l_send, l_recv, row, plane_peer(col, k)).start())

    def along_cols(buf, send_sem, recv_sem):
        for n, shift in enumerate(SHIFTS):
            @pl.when(on_map(col + shift))
            def _():
                remote(
                    buf.at[7], buf.at[7 - shift], send_sem.at[n], recv_sem.at[n], row, col + shift
                ).start()

            @pl.when(jnp.logical_not(on_map(col - shift)))
            def _():
                buf[7 - shift] = jnp.zeros((128, 128), BF)

    def wait_cols(buf, send_sem, recv_sem):
        for n, shift in enumerate(SHIFTS):
            @pl.when(on_map(col - shift))
            def _():
                wait_bytes(buf.at[7], recv_sem.at[n])
        for n, shift in enumerate(SHIFTS):
            @pl.when(on_map(col + shift))
            def _():
                wait_bytes(buf.at[7], send_sem.at[n])

    def along_rows(buf, send_sem, recv_sem):
        band = buf.at[pl.ds(5, 5)]
        none = jnp.zeros((5, 128, 128), BF)

        @pl.when(row < ROWS - 1)
        def _():
            remote(band, buf.at[pl.ds(0, 5)], send_sem.at[0], recv_sem.at[0], row + 1, col).start()

        @pl.when(row > 0)
        def _():
            remote(band, buf.at[pl.ds(10, 5)], send_sem.at[1], recv_sem.at[1], row - 1, col).start()

        @pl.when(row == 0)
        def _():
            buf[pl.ds(0, 5)] = none

        @pl.when(row == ROWS - 1)
        def _():
            buf[pl.ds(10, 5)] = none

    def wait_rows(buf, send_sem, recv_sem):
        @pl.when(row < ROWS - 1)
        def _():
            wait_bytes(buf.at[pl.ds(5, 5)], send_sem.at[0])
            wait_bytes(buf.at[pl.ds(10, 5)], recv_sem.at[1])

        @pl.when(row > 0)
        def _():
            wait_bytes(buf.at[pl.ds(5, 5)], send_sem.at[1])
            wait_bytes(buf.at[pl.ds(0, 5)], recv_sem.at[0])

    with jax.named_scope("relay"):
        def relay(k):
            p = lax.rem(row + ROWS - 2 * k, 8)
            block = right.at[pl.ds(4 * p, 4)]
            wait_bytes(block, r_relay.at[p // 2])
            remote(block, block, r_send, r_recv, sibling, col).start()

        each(1, 4, relay)
    along_cols(cots, c_send, c_recv)

    with jax.named_scope("cotangent"):
        for n in range(4, 10):
            loads[n].wait()
        gating = jax.nn.sigmoid(jnp.dot(normed, wgate_v[...], preferred_element_type=F32))

    one_rate = rates_s[0]
    two_rate = rates_s[1]
    to = lax.broadcasted_iota(jnp.int32, (128, 128), 0)
    at = lax.broadcasted_iota(jnp.int32, (128, 128), 1)
    flip = ((lax.rem(to, 16) * 8 + to // 16) == at).astype(BF)
    flip_back = ((lax.rem(to, 8) * 16 + to // 8) == at).astype(BF)

    def unfold(src, dst, blocks):
        for n in blocks:
            dr, dc = n // 5 - 1, n % 5 - 2
            inside = (row + dr >= 0) & (row + dr < ROWS) & (col + dc >= 0) & (col + dc < COLS)
            cell = jnp.dot(flip, src[n], preferred_element_type=F32)
            dst[pl.ds((dc + 2) * 8, 8), pl.ds((dr + 1) * 16, 16), :] = jnp.where(
                inside, cell, 0.0
            ).reshape(8, 16, 128)

    def back(value):
        return jnp.dot(flip_back, value, preferred_element_type=F32).astype(BF)

    with jax.named_scope("gatherwait"):
        wait_bytes(right.at[pl.ds(0, 16)], r_recv)
    with jax.named_scope("leftwait"):
        wait_bytes(left.at[pl.ds(0, 30)], l_recv)
        wait_cols(cots, c_send, c_recv)
        along_rows(cots, c_send2, c_recv2)

    with jax.named_scope("products"):
        for part in range(4):
            def add(c, total):
                a = left[c, pl.ds(part * 32, 32), :].astype(F32).reshape(4, 1, 8, 128)
                b = right[c].astype(F32).reshape(1, 8, 8, 128)
                return total + a * b

            total = lax.fori_loop(0, COLS, add, jnp.zeros((4, 8, 8, 128), F32))
            sums[pl.ds(part * 32, 32), :] = jnp.sum(total, axis=2).reshape(32, 128)

    with jax.named_scope("update"):
        product_norm = layer_norm(sums[...]).astype(BF)
        updated = (
            pair + gating * jnp.dot(product_norm, wout_v[...], preferred_element_type=F32)
        ).astype(BF).astype(F32)
        contact = mask_column(cmask_v[...])
        centre = updated - jnp.mean(updated, axis=-1, keepdims=True)
        inv = lax.rsqrt(jnp.mean(centre * centre, axis=-1, keepdims=True) + EPSILON)
        scaled = centre * inv
        first[7] = (scaled * contact).astype(BF)
    with jax.named_scope("rimcols"):
        along_cols(first, f_send, f_recv)
        wait_rows(cots, c_send2, c_recv2)
    with jax.named_scope("hidden"):
        unfold(cots, cfield, range(15))
        shifted(cfield, ctaps, 8, two_rate, 32, -1)
        back_two = jnp.concatenate([two_v[t].T for t in range(9)], axis=0)
        ghid[...] = jnp.dot(
            windows(ctaps, 8, two_rate, 24, -1), back_two, preferred_element_type=F32
        )
    with jax.named_scope("rimwait"):
        wait_cols(first, f_send, f_recv)
        along_rows(first, f_send2, f_recv2)
    with jax.named_scope("rimrows"):
        unfold(first, field, range(5, 10))
        wait_rows(first, f_send2, f_recv2)
    with jax.named_scope("unfold"):
        unfold(first, field, [*range(5), *range(10, 15)])
        shifted(field, taps, 8, one_rate, 32, 1)
    with jax.named_scope("conv"):
        pre = jnp.dot(
            windows(taps, 8, one_rate, 24, 1), one_v[...].reshape(1152, 128),
            preferred_element_type=F32,
        )
        c_at = lax.broadcasted_iota(jnp.int32, (24, 32, 128), 0) + (col * 8 - 8)
        r_at = lax.broadcasted_iota(jnp.int32, (24, 32, 128), 1) + (row * 16 - 8)
        inside = (c_at >= 0) & (c_at < 256) & (r_at >= 0) & (r_at < 256)
        sigma = jax.nn.sigmoid(pre)
        hidden[...] = jnp.where(inside, (pre * sigma).reshape(24, 32, 128), 0.0)
        gpre[...] = jnp.where(
            inside, (ghid[...] * sigma * (1.0 + pre * (1.0 - sigma))).reshape(24, 32, 128), 0.0
        )
        shifted(hidden, htaps, 8, two_rate, 16, 1)
    over = (((0,), (0,)), ((), ()))

    def scatter(k, low):
        peer = plane_peer(col, k)
        slot = plane_slot(peer)

        @pl.when((slot >= low) & (slot < low + 8))
        def _():
            remote(grads.at[slot], parts.at[me], send1, recv1, row, peer).start()

    with jax.named_scope("gradtwo"):
        cot_own = cots[7]
        second_taps = back(windows(htaps, 8, two_rate, 8, 1))
        grads[pl.ds(8, 8)] = lax.dot_general(
            second_taps, cot_own, over, preferred_element_type=F32
        ).astype(BF).reshape(8, 144, 128)
        each(1, 16, lambda k: scatter(k, 8))
    with jax.named_scope("gradone"):
        gpre_own = gpre[pl.ds(8, 8), pl.ds(8, 16), :].reshape(128, 128).astype(BF)
        first_taps = windows(taps, 16, one_rate, 8, 1, pl.ds(8, 16))
        grads[pl.ds(0, 8)] = lax.dot_general(
            first_taps, gpre_own, over, preferred_element_type=F32
        ).astype(BF).reshape(8, 144, 128)
        each(1, 16, lambda k: scatter(k, 0))
    with jax.named_scope("outputs"):
        parts[me] = grads[me]
        second_pre = jnp.dot(
            second_taps, two_v[...].reshape(1152, 128), preferred_element_type=F32
        )
        output_ref[...] = (updated + second_pre).astype(BF)
        shifted(gpre, gtaps, 8, one_rate, 16, -1)
        back_one = jnp.concatenate([one_v[t].T for t in range(9)], axis=0)
        grad_in = contact * jnp.dot(
            back(windows(gtaps, 8, one_rate, 8, -1)), back_one, preferred_element_type=F32
        )
        grad_norm = inv * (
            grad_in
            - jnp.mean(grad_in, axis=-1, keepdims=True)
            - scaled * jnp.mean(grad_in * scaled, axis=-1, keepdims=True)
        )
        gpair_ref[...] = (cot_own.astype(F32) + grad_norm).astype(BF)

    most = parts.at[pl.ds(0, 15)]
    with jax.named_scope("scatterwait"):
        wait_bytes(most, recv1)
    with jax.named_scope("addparts"):
        total = parts[0].astype(F32)
        for n in range(1, 16):
            total = total + parts[n].astype(F32)
        own[...] = total.astype(BF).reshape(9, 16, 128)
        for j in range(9):
            @pl.when(place != 3 * j)
            def _():
                remote(own.at[j], pieces.at[place], send2, recv2, *line(3 * j)).start()

    owner = (lax.rem(place, 3) == 0) & (place < 27)
    piece = place // 3

    with jax.named_scope("line"):
        @pl.when(owner)
        def _():
            pieces[place] = own[piece]
            wait_bytes(own.at[pl.ds(0, 8)], send2)
            wait_bytes(pieces.at[pl.ds(0, 31)], recv2)
            total = pieces[0].astype(F32)
            for n in range(1, 32):
                total = total + pieces[n].astype(F32)
            final[me, piece] = total.astype(BF)
            block = final.at[me, piece]
            each(1, 32, lambda k: remote(
                block, block, send3, recv3, *line(lax.rem(place + k, 32))).start())
            wait_bytes(own.at[pl.ds(0, 8)], recv3)

        @pl.when(jnp.logical_not(owner))
        def _():
            wait_bytes(own, send2)
            wait_bytes(own, recv3)

    with jax.named_scope("gather"):
        whole = final.at[me]
        each(1, 16, lambda k: remote(whole, whole, send4, recv4, row, plane_peer(col, k)).start())
        wait_bytes(right.at[pl.ds(0, 28)], r_send)
        wait_bytes(left.at[pl.ds(0, 31)], l_send)
        wait_bytes(most, send1)

        @pl.when(owner)
        def _():
            wait_bytes(pieces.at[pl.ds(0, 31)], send3)

        wait_bytes(final.at[pl.ds(0, 15)], recv4)
    with jax.named_scope("finish"):
        wait_bytes(final.at[pl.ds(0, 15)], send4)
        total_ref[...] = final[...].reshape(16, 144, 128)


VMEM = pltpu.VMEM
DMA = pltpu.SemaphoreType.DMA


def shape(dims, dtype):
    return jax.ShapeDtypeStruct(dims, dtype)


def local(
    pair, pair_mask, contact_mask, dilations, w_proj, w_gate, w_out, conv_one, conv_two, cotangent
):
    inputs = (
        pair.reshape(128, 128), pair_mask.T, contact_mask.T, dilations, w_proj, w_gate, w_out,
        conv_one, conv_two, cotangent.reshape(128, 128),
    )
    output, grad_pair, total = pl.pallas_call(
        kernel,
        out_shape=(shape((128, 128), BF), shape((128, 128), BF), shape((16, 144, 128), BF)),
        in_specs=[pl.BlockSpec(memory_space=pltpu.HBM)] * 10,
        out_specs=(pl.BlockSpec(memory_space=pltpu.VMEM),) * 3,
        scratch_shapes=[
            VMEM((128, 128), BF), VMEM((8, 16), jnp.int32), VMEM((8, 16), jnp.int32),
            pltpu.SMEM((2,), jnp.int32), VMEM((128, 512), BF), VMEM((128, 128), BF),
            VMEM((128, 128), BF), VMEM((9, 128, 128), BF), VMEM((9, 128, 128), BF), DMA((10,)),
            VMEM((32, 128, 128), BF), VMEM((32, 64, 128), BF), VMEM((2, 64, 128), BF),
            VMEM((15, 128, 128), BF), VMEM((15, 128, 128), BF), VMEM((128, 128), F32),
            VMEM((40, 48, 128), F32), VMEM((3, 40, 32, 128), BF),
            VMEM((40, 48, 128), F32), VMEM((3, 40, 32, 128), BF),
            VMEM((24, 32, 128), F32), VMEM((3, 24, 16, 128), BF),
            VMEM((24, 32, 128), F32), VMEM((3, 24, 16, 128), BF), VMEM((768, 128), F32),
            VMEM((16, 144, 128), BF), VMEM((16, 144, 128), BF), VMEM((9, 16, 128), BF),
            VMEM((32, 16, 128), BF), VMEM((16, 9, 16, 128), BF),
            DMA, DMA, DMA, DMA((4,)), DMA((4,)), DMA, DMA, DMA((4,)),
            DMA((4,)), DMA((4,)), DMA((2,)), DMA((2,)),
            DMA((4,)), DMA((4,)), DMA((2,)), DMA((2,)),
            DMA, DMA, DMA, DMA, DMA, DMA, DMA, DMA,
        ],
        compiler_params=pltpu.CompilerParams(
            collective_id=1, has_side_effects=True, vmem_limit_bytes=62 << 20
        ),
    )(*inputs)
    total = total.reshape(2, 9, 128, 128).astype(F32) * (1.0 / 256.0)
    return (output.reshape(16, 8, 128), grad_pair.reshape(16, 8, 128), total[0], total[1])


def solution(mesh):
    in_specs = (
        P("row", "col", None), P("row", "col"), P("row", "col"), P(), P(), P(), P(), P(), P(),
        P("row", "col", None),
    )
    out_specs = (P("row", "col", None), P("row", "col", None), P(), P())
    return jax.shard_map(local, mesh=mesh, in_specs=in_specs, out_specs=out_specs, check_vma=False)
```

```python
import jax
import jax.numpy as jnp
from jax import lax
from jax.experimental import pallas as pl
from jax.experimental.pallas import tpu as pltpu
from jax.sharding import PartitionSpec as P

EPSILON = 1e-05
MESH = pl.DeviceIdType.MESH
BF = jnp.bfloat16
F32 = jnp.float32
ROWS = 16
COLS = 32
SHIFTS = (1, 2, -1, -2)


def signal(sem, row, col):
    pl.semaphore_signal(sem, inc=1, device_id=(row, col), device_id_type=MESH)


def remote(src, dst, send_sem, recv_sem, row, col):
    return pltpu.make_async_remote_copy(
        src_ref=src,
        dst_ref=dst,
        send_sem=send_sem,
        recv_sem=recv_sem,
        device_id=(row, col),
        device_id_type=MESH,
    )


def wait_bytes(ref, sem):
    pltpu.make_async_copy(ref, ref, sem).wait()


def each(low, high, body):
    def step(k, carry):
        body(k)
        return carry

    lax.fori_loop(low, high, step, 0)


def plane_peer(col, k):
    x = lax.rem(col // 8 + k // 4, 4)
    y = lax.rem(lax.rem(col, 4) + lax.rem(k, 4), 4)
    return x * 8 + lax.rem(col // 4, 2) * 4 + y


def plane_slot(col):
    return (col // 8) * 4 + lax.rem(col, 4)


def on_map(col):
    return (col >= 0) & (col < COLS)


def layer_norm(values):
    centre = values - jnp.mean(values, axis=-1, keepdims=True)
    spread = jnp.mean(centre * centre, axis=-1, keepdims=True)
    return centre * lax.rsqrt(spread + EPSILON)


def mask_column(mask):
    pix = lax.broadcasted_iota(jnp.int32, (128, 8), 0)
    lane = lax.broadcasted_iota(jnp.int32, (128, 8), 1)
    pick = (lax.rem(pix, 8) == lane).astype(F32)
    spread = jnp.dot(pick, mask.astype(F32), preferred_element_type=F32)
    place = lax.broadcasted_iota(jnp.int32, (128, 16), 0) // 8
    at = lax.broadcasted_iota(jnp.int32, (128, 16), 1)
    return jnp.sum(jnp.where(place == at, spread, 0.0), axis=1, keepdims=True)


def shifted(src, dst, start, rate, length, sign):
    wide = src.shape[1]
    for r in range(3):
        move = lax.rem(2 * wide - (start + sign * (r - 1) * rate), wide)
        dst[r] = pltpu.roll(src[...], move, 1)[:, :length].astype(BF)


def windows(src, start, rate, count, sign, rows=None):
    found = []
    for t in range(9):
        at = pl.ds(start + sign * (t % 3 - 1) * rate, count)
        piece = src[t // 3, at] if rows is None else src[t // 3, at, rows, :]
        found.append(piece.reshape(-1, 128))
    return jnp.concatenate(found, axis=1)


def kernel(
    pair_h, pmask_h, cmask_h, rates_h, wproj_h, wgate_h, wout_h, one_h, two_h, cot_h,
    output_ref, gpair_ref, total_ref,
    pair_v, pmask_v, cmask_v, rates_s, wproj_v, wgate_v, wout_v, one_v, two_v, in_sem,
    left, right, halves, first, cots, sums,
    field, taps, cfield, ctaps, hidden, htaps, gpre, gtaps, ghid,
    grads, parts, near, apart, final, partial,
    l_send, l_recv, l_recv2, l_far, r_send0, r_recv0, r_send, r_recv, r_relay,
    c_send, c_recv, c_send2, c_recv2, f_send, f_recv, f_send2, f_recv2,
    send1, recv1, send2, recv2, send3, recv3, send4, recv4, recv5,
):
    row = lax.axis_index("row")
    col = lax.axis_index("col")
    far = (col // 8) * 8 + (1 - lax.rem(col // 4, 2)) * 4 + lax.rem(col, 4)
    sibling = row + 1 - 2 * lax.rem(row, 2)
    turn_row = col // 2
    turn_col = 4 * lax.rem(row, 8)
    core = lax.rem(row, 2)
    z_hi = lax.rem(col // 4, 2)
    near_place = lax.rem(row // 2, 4)
    far_place = z_hi * 2 + row // 8
    me = core * 16 + plane_slot(col)

    def near_row(k):
        return (row // 8) * 8 + lax.rem(row + 2 * k, 8)

    def far_at(k):
        z = lax.rem(z_hi * 8 + row // 2 + 4 * k, 16)
        return lax.rem(z, 8) * 2 + core, (col // 8) * 8 + (z // 8) * 4 + lax.rem(col, 4)

    with jax.named_scope("start"):
        loads = [
            pltpu.make_async_copy(src, dst, in_sem.at[n])
            for n, (src, dst) in enumerate((
                (pair_h, pair_v), (pmask_h, pmask_v), (wproj_h, wproj_v), (cot_h, cots.at[7]),
                (wgate_h, wgate_v), (wout_h, wout_v), (cmask_h, cmask_v), (rates_h, rates_s),
                (two_h, two_v), (one_h, one_v),
            ))
        ]
        for load in loads:
            load.start()
        barrier = pltpu.get_barrier_semaphore()
        each(0, 16, lambda k: signal(barrier, sibling, plane_peer(col, k)))
        each(1, 16, lambda k: signal(barrier, row, plane_peer(col, k)))
        for k in range(1, 4):
            signal(barrier, near_row(k), col)
            signal(barrier, *far_at(k))
        beside = row + 2 * core - 1

        @pl.when((beside >= 0) & (beside < ROWS))
        def _():
            signal(barrier, beside, col)

        for shift in (1, 2, -1, -2):
            @pl.when(on_map(col + shift))
            def _():
                signal(barrier, row, col + shift)
        for n in range(4):
            @pl.when((turn_row != row) | (turn_col + n != col))
            def _():
                signal(barrier, turn_row, turn_col + n)

    with jax.named_scope("project"):
        for n in (0, 1, 2):
            loads[n].wait()
        pair = pair_v[...].astype(F32)
        normed = layer_norm(pair).astype(BF)
        projected = jnp.dot(normed, wproj_v[...], preferred_element_type=F32)
        mask = mask_column(pmask_v[...])
        left[col] = (mask * jax.nn.sigmoid(projected[:, 128:256]) * projected[:, :128]).astype(BF)
        halves[...] = (
            (mask * jax.nn.sigmoid(projected[:, 384:]) * projected[:, 256:384])
            .astype(BF)
            .reshape(2, 64, 128)
        )
        loads[3].wait()

    with jax.named_scope("barrier"):
        fixed = (turn_row == row) & (lax.rem(row, 8) == col // 4)
        pl.semaphore_wait(
            barrier,
            41
            - jnp.where(fixed, 1, 0)
            + jnp.where((beside >= 0) & (beside < ROWS), 1, 0)
            + jnp.minimum(col, 2)
            + jnp.minimum(COLS - 1 - col, 2),
        )

    with jax.named_scope("turn"):
        def turn(half, low):
            return low * 8 + col // 4, 2 * row + half

        for half in range(2):
            for low in range(2):
                t_row, t_col = turn(half, low)

                @pl.when((t_row != row) | (t_col != col))
                def _():
                    remote(
                        halves.at[half], right.at[col], r_send0.at[2 * half + low],
                        r_recv0.at[lax.rem(col, 4)], t_row, t_col,
                    ).start()

                @pl.when((t_row == row) & (t_col == col))
                def _():
                    right[col] = halves[half]

        mine = left.at[col]
        remote(mine, mine, l_send, l_far, row, far).start()
        each(1, 16, lambda k: remote(mine, mine, l_send, l_recv, row, plane_peer(col, k)).start())

        for half in range(2):
            for low in range(2):
                t_row, t_col = turn(half, low)

                @pl.when((t_row != row) | (t_col != col))
                def _():
                    wait_bytes(halves.at[half], r_send0.at[2 * half + low])
        for n in range(4):
            @pl.when((turn_row != row) | (turn_col + n != col))
            def _():
                wait_bytes(right.at[0], r_recv0.at[n])

    with jax.named_scope("spread"):
        four = right.at[pl.ds(turn_col, 4)]
        each(1, 4, lambda k: remote(
            four, four, r_send, r_relay.at[lax.rem(row, 8) // 2],
            (row // 8) * 8 + lax.rem(row + 2 * k, 8), col).start())
        remote(four, four, r_send, r_recv, sibling, col).start()

    with jax.named_scope("farwait"):
        far_block = left.at[far]
        wait_bytes(far_block, l_far)
        each(1, 16, lambda k: remote(
            far_block, far_block, l_send, l_recv2, row, plane_peer(col, k)).start())

    def along_cols(buf, send_sem, recv_sem):
        for n, shift in enumerate(SHIFTS):
            @pl.when(on_map(col + shift))
            def _():
                remote(
                    buf.at[7], buf.at[7 - shift], send_sem.at[n], recv_sem.at[n], row, col + shift
                ).start()

            @pl.when(jnp.logical_not(on_map(col - shift)))
            def _():
                buf[7 - shift] = jnp.zeros((128, 128), BF)

    def wait_cols(buf, send_sem, recv_sem):
        for n, shift in enumerate(SHIFTS):
            @pl.when(on_map(col - shift))
            def _():
                wait_bytes(buf.at[7], recv_sem.at[n])
        for n, shift in enumerate(SHIFTS):
            @pl.when(on_map(col + shift))
            def _():
                wait_bytes(buf.at[7], send_sem.at[n])

    def along_rows(buf, send_sem, recv_sem):
        band = buf.at[pl.ds(5, 5)]
        none = jnp.zeros((5, 128, 128), BF)

        @pl.when(row < ROWS - 1)
        def _():
            remote(band, buf.at[pl.ds(0, 5)], send_sem.at[0], recv_sem.at[0], row + 1, col).start()

        @pl.when(row > 0)
        def _():
            remote(band, buf.at[pl.ds(10, 5)], send_sem.at[1], recv_sem.at[1], row - 1, col).start()

        @pl.when(row == 0)
        def _():
            buf[pl.ds(0, 5)] = none

        @pl.when(row == ROWS - 1)
        def _():
            buf[pl.ds(10, 5)] = none

    def wait_rows(buf, send_sem, recv_sem):
        @pl.when(row < ROWS - 1)
        def _():
            wait_bytes(buf.at[pl.ds(5, 5)], send_sem.at[0])
            wait_bytes(buf.at[pl.ds(10, 5)], recv_sem.at[1])

        @pl.when(row > 0)
        def _():
            wait_bytes(buf.at[pl.ds(5, 5)], send_sem.at[1])
            wait_bytes(buf.at[pl.ds(0, 5)], recv_sem.at[0])

    with jax.named_scope("relay"):
        def relay(k):
            p = lax.rem(row + ROWS - 2 * k, 8)
            block = right.at[pl.ds(4 * p, 4)]
            wait_bytes(block, r_relay.at[p // 2])
            remote(block, block, r_send, r_recv, sibling, col).start()

        each(1, 4, relay)
    along_cols(cots, c_send, c_recv)

    with jax.named_scope("cotangent"):
        for n in range(4, 10):
            loads[n].wait()
        gating = jax.nn.sigmoid(jnp.dot(normed, wgate_v[...], preferred_element_type=F32))

    one_rate = rates_s[0]
    two_rate = rates_s[1]
    to = lax.broadcasted_iota(jnp.int32, (128, 128), 0)
    at = lax.broadcasted_iota(jnp.int32, (128, 128), 1)
    flip = ((lax.rem(to, 16) * 8 + to // 16) == at).astype(BF)
    flip_back = ((lax.rem(to, 8) * 16 + to // 8) == at).astype(BF)

    def unfold(src, dst, blocks):
        for n in blocks:
            dr, dc = n // 5 - 1, n % 5 - 2
            inside = (row + dr >= 0) & (row + dr < ROWS) & (col + dc >= 0) & (col + dc < COLS)
            cell = jnp.dot(flip, src[n], preferred_element_type=F32)
            dst[pl.ds((dc + 2) * 8, 8), pl.ds((dr + 1) * 16, 16), :] = jnp.where(
                inside, cell, 0.0
            ).reshape(8, 16, 128)

    def back(value):
        return jnp.dot(flip_back, value, preferred_element_type=F32).astype(BF)

    sibling_part = right.at[pl.ds(0, 16)]

    def add_from(half, part, total):
        def add(n, total):
            c = (n // 4) * 8 + half * 4 + lax.rem(n, 4)
            a = left[c, pl.ds(part * 32, 32), :].astype(F32).reshape(4, 1, 8, 128)
            b = right[c].astype(F32).reshape(1, 8, 8, 128)
            return total + a * b

        return lax.fori_loop(0, 16, add, total)

    with jax.named_scope("products"):
        @pl.when(core != z_hi)
        def _():
            wait_bytes(sibling_part, r_recv)

        wait_bytes(left.at[pl.ds(0, 15)], l_recv)
        for part in range(4):
            partial[part] = add_from(z_hi, part, jnp.zeros((4, 8, 8, 128), F32))
        wait_bytes(left.at[pl.ds(0, 15)], l_recv2)

        @pl.when(core == z_hi)
        def _():
            wait_bytes(sibling_part, r_recv)

        wait_cols(cots, c_send, c_recv)
        along_rows(cots, c_send2, c_recv2)
        for part in range(4):
            total = add_from(1 - z_hi, part, partial[part])
            sums[pl.ds(part * 32, 32), :] = jnp.sum(total, axis=2).reshape(32, 128)

    with jax.named_scope("update"):
        product_norm = layer_norm(sums[...]).astype(BF)
        updated = (
            pair + gating * jnp.dot(product_norm, wout_v[...], preferred_element_type=F32)
        ).astype(BF).astype(F32)
        contact = mask_column(cmask_v[...])
        centre = updated - jnp.mean(updated, axis=-1, keepdims=True)
        inv = lax.rsqrt(jnp.mean(centre * centre, axis=-1, keepdims=True) + EPSILON)
        scaled = centre * inv
        first[7] = (scaled * contact).astype(BF)
    with jax.named_scope("rimcols"):
        along_cols(first, f_send, f_recv)
        wait_rows(cots, c_send2, c_recv2)
    with jax.named_scope("hidden"):
        unfold(cots, cfield, range(15))
        shifted(cfield, ctaps, 8, two_rate, 32, -1)
        back_two = jnp.concatenate([two_v[t].T for t in range(9)], axis=0)
        ghid[...] = jnp.dot(
            windows(ctaps, 8, two_rate, 24, -1), back_two, preferred_element_type=F32
        )
    with jax.named_scope("rimwait"):
        wait_cols(first, f_send, f_recv)
        along_rows(first, f_send2, f_recv2)
    with jax.named_scope("rimrows"):
        unfold(first, field, range(5, 10))
        wait_rows(first, f_send2, f_recv2)
    with jax.named_scope("unfold"):
        unfold(first, field, [*range(5), *range(10, 15)])
        shifted(field, taps, 8, one_rate, 32, 1)
    with jax.named_scope("conv"):
        pre = jnp.dot(
            windows(taps, 8, one_rate, 24, 1), one_v[...].reshape(1152, 128),
            preferred_element_type=F32,
        )
        c_at = lax.broadcasted_iota(jnp.int32, (24, 32, 128), 0) + (col * 8 - 8)
        r_at = lax.broadcasted_iota(jnp.int32, (24, 32, 128), 1) + (row * 16 - 8)
        inside = (c_at >= 0) & (c_at < 256) & (r_at >= 0) & (r_at < 256)
        sigma = jax.nn.sigmoid(pre)
        hidden[...] = jnp.where(inside, (pre * sigma).reshape(24, 32, 128), 0.0)
        gpre[...] = jnp.where(
            inside, (ghid[...] * sigma * (1.0 + pre * (1.0 - sigma))).reshape(24, 32, 128), 0.0
        )
        shifted(hidden, htaps, 8, two_rate, 16, 1)
    over = (((0,), (0,)), ((), ()))

    def scatter(there):
        def one(k):
            peer = plane_peer(col, k)

            @pl.when((k > 0) | (there != core))
            def _():
                remote(
                    grads.at[there * 16 + plane_slot(peer)], parts.at[me], send1, recv1,
                    row - core + there, peer,
                ).start()

        each(0, 16, one)

    def padded(value):
        return jnp.concatenate([value.astype(BF), jnp.zeros((128, 128), BF)]).reshape(16, 80, 128)

    with jax.named_scope("gradtwo"):
        cot_own = cots[7]
        second_taps = back(windows(htaps, 8, two_rate, 8, 1))
        grads[pl.ds(16, 16)] = padded(
            lax.dot_general(second_taps, cot_own, over, preferred_element_type=F32)
        )
        scatter(1)
    with jax.named_scope("gradone"):
        gpre_own = gpre[pl.ds(8, 8), pl.ds(8, 16), :].reshape(128, 128).astype(BF)
        first_taps = windows(taps, 16, one_rate, 8, 1, pl.ds(8, 16))
        grads[pl.ds(0, 16)] = padded(
            lax.dot_general(first_taps, gpre_own, over, preferred_element_type=F32)
        )
        scatter(0)
    with jax.named_scope("outputs"):
        parts[me] = grads[me]
        second_pre = jnp.dot(
            second_taps, two_v[...].reshape(1152, 128), preferred_element_type=F32
        )
        output_ref[...] = (updated + second_pre).astype(BF)
        shifted(gpre, gtaps, 8, one_rate, 16, -1)
        back_one = jnp.concatenate([one_v[t].T for t in range(9)], axis=0)
        grad_in = contact * jnp.dot(
            back(windows(gtaps, 8, one_rate, 8, -1)), back_one, preferred_element_type=F32
        )
        grad_norm = inv * (
            grad_in
            - jnp.mean(grad_in, axis=-1, keepdims=True)
            - scaled * jnp.mean(grad_in * scaled, axis=-1, keepdims=True)
        )
        gpair_ref[...] = (cot_own.astype(F32) + grad_norm).astype(BF)

    def added(buf, count):
        total = buf[0].astype(F32)
        for n in range(1, count):
            total = total + buf[n].astype(F32)
        return total.astype(BF)

    most = parts.at[pl.ds(0, 31)]
    three = near.at[pl.ds(0, 3)]
    with jax.named_scope("scatterwait"):
        wait_bytes(most, recv1)
    with jax.named_scope("near"):
        near[near_place] = added(parts, 32)
        block = near.at[near_place]
        for k in range(1, 4):
            remote(block, block, send2, recv2, near_row(k), col).start()
        wait_bytes(three, recv2)
    with jax.named_scope("apart"):
        apart[far_place] = added(near, 4)
        block_far = apart.at[far_place]
        for k in (2, 1, 3):
            remote(block_far, block_far, send3, recv3, *far_at(k)).start()
        wait_bytes(three, recv3)
    with jax.named_scope("gather"):
        final[me] = added(apart, 4)
        whole = final.at[me]
        each(1, 16, lambda k: remote(
            whole, whole, send4, recv4.at[plane_slot(col)], row, plane_peer(col, k)).start())
        remote(whole, whole, send4, recv5, sibling, col).start()

        def hand_on(k):
            slot = plane_slot(plane_peer(col, k))
            block = final.at[core * 16 + slot]
            wait_bytes(block, recv4.at[slot])
            remote(block, block, send4, recv5, sibling, col).start()

        each(1, 16, hand_on)
        wait_bytes(right.at[pl.ds(0, 28)], r_send)
        wait_bytes(left.at[pl.ds(0, 31)], l_send)
        wait_bytes(most, send1)
        wait_bytes(three, send2)
        wait_bytes(three, send3)
        wait_bytes(final.at[pl.ds(0, 16)], recv5)
    with jax.named_scope("finish"):
        wait_bytes(most, send4)
        total_ref[...] = final[...]


def finish_kernel(output_in, gpair_in, total_in, output_ref, gpair_ref, one_ref, two_ref):
    output_ref[...] = output_in[...]
    gpair_ref[...] = gpair_in[...]
    for half, ref in enumerate((one_ref, two_ref)):
        grad = total_in[pl.ds(16 * half, 16)].reshape(1280, 128)[:1152].astype(F32)
        ref[...] = (grad * (1.0 / 256.0)).reshape(9, 128, 128)


VMEM = pltpu.VMEM
DMA = pltpu.SemaphoreType.DMA


def shape(dims, dtype):
    return jax.ShapeDtypeStruct(dims, dtype)


def local(
    pair, pair_mask, contact_mask, dilations, w_proj, w_gate, w_out, conv_one, conv_two, cotangent
):
    inputs = (
        pair.reshape(128, 128), pair_mask.T, contact_mask.T, dilations, w_proj, w_gate, w_out,
        conv_one, conv_two, cotangent.reshape(128, 128),
    )
    output, grad_pair, total = pl.pallas_call(
        kernel,
        out_shape=(shape((128, 128), BF), shape((128, 128), BF), shape((32, 80, 128), BF)),
        in_specs=[pl.BlockSpec(memory_space=pltpu.HBM)] * 10,
        out_specs=(pl.BlockSpec(memory_space=pltpu.VMEM),) * 3,
        scratch_shapes=[
            VMEM((128, 128), BF), VMEM((8, 16), jnp.int32), VMEM((8, 16), jnp.int32),
            pltpu.SMEM((2,), jnp.int32), VMEM((128, 512), BF), VMEM((128, 128), BF),
            VMEM((128, 128), BF), VMEM((9, 128, 128), BF), VMEM((9, 128, 128), BF), DMA((10,)),
            VMEM((32, 128, 128), BF), VMEM((32, 64, 128), BF), VMEM((2, 64, 128), BF),
            VMEM((15, 128, 128), BF), VMEM((15, 128, 128), BF), VMEM((128, 128), F32),
            VMEM((40, 48, 128), F32), VMEM((3, 40, 32, 128), BF),
            VMEM((40, 48, 128), F32), VMEM((3, 40, 32, 128), BF),
            VMEM((24, 32, 128), F32), VMEM((3, 24, 16, 128), BF),
            VMEM((24, 32, 128), F32), VMEM((3, 24, 16, 128), BF), VMEM((768, 128), F32),
            VMEM((32, 80, 128), BF), VMEM((32, 80, 128), BF), VMEM((4, 80, 128), BF),
            VMEM((4, 80, 128), BF), VMEM((32, 80, 128), BF), VMEM((4, 4, 8, 8, 128), F32),
            DMA, DMA, DMA, DMA, DMA((4,)), DMA((4,)), DMA, DMA, DMA((4,)),
            DMA((4,)), DMA((4,)), DMA((2,)), DMA((2,)),
            DMA((4,)), DMA((4,)), DMA((2,)), DMA((2,)),
            DMA, DMA, DMA, DMA, DMA, DMA, DMA, DMA((16,)), DMA,
        ],
        compiler_params=pltpu.CompilerParams(
            collective_id=1, has_side_effects=True, vmem_limit_bytes=62 << 20
        ),
    )(*inputs)
    whole = pl.BlockSpec(memory_space=pltpu.VMEM)
    output, grad_pair, grad_one, grad_two = pl.pallas_call(
        finish_kernel,
        out_shape=(
            shape((128, 128), BF), shape((128, 128), BF),
            shape((9, 128, 128), F32), shape((9, 128, 128), F32),
        ),
        in_specs=[whole] * 3,
        out_specs=(whole,) * 4,
    )(output, grad_pair, total)
    return (output.reshape(16, 8, 128), grad_pair.reshape(16, 8, 128), grad_one, grad_two)


def solution(mesh):
    in_specs = (
        P("row", "col", None), P("row", "col"), P("row", "col"), P(), P(), P(), P(), P(), P(),
        P("row", "col", None),
    )
    out_specs = (P("row", "col", None), P("row", "col", None), P(), P())
    return jax.shard_map(local, mesh=mesh, in_specs=in_specs, out_specs=out_specs, check_vma=False)
```

```python
import jax
import jax.numpy as jnp
from jax import lax
from jax.experimental import pallas as pl
from jax.experimental.pallas import tpu as pltpu
from jax.sharding import PartitionSpec as P

EPSILON = 1e-05
MESH = pl.DeviceIdType.MESH
BF = jnp.bfloat16
F32 = jnp.float32
ROWS = 16
COLS = 32
CHUNKS = (pl.ds(0, 48), pl.ds(48, 32))
SHIFTS = (1, 2, -1, -2)


def signal(sem, row, col):
    pl.semaphore_signal(sem, inc=1, device_id=(row, col), device_id_type=MESH)


def remote(src, dst, send_sem, recv_sem, row, col):
    return pltpu.make_async_remote_copy(
        src_ref=src,
        dst_ref=dst,
        send_sem=send_sem,
        recv_sem=recv_sem,
        device_id=(row, col),
        device_id_type=MESH,
    )


def wait_bytes(ref, sem):
    pltpu.make_async_copy(ref, ref, sem).wait()


def each(low, high, body):
    def step(k, carry):
        body(k)
        return carry

    lax.fori_loop(low, high, step, 0)


def plane_peer(col, k):
    x = lax.rem(col // 8 + k // 4, 4)
    y = lax.rem(lax.rem(col, 4) + lax.rem(k, 4), 4)
    return x * 8 + lax.rem(col // 4, 2) * 4 + y


def plane_slot(col):
    return (col // 8) * 4 + lax.rem(col, 4)


def on_map(col):
    return (col >= 0) & (col < COLS)


def layer_norm(values):
    centre = values - jnp.mean(values, axis=-1, keepdims=True)
    spread = jnp.mean(centre * centre, axis=-1, keepdims=True)
    return centre * lax.rsqrt(spread + EPSILON)


def mask_column(mask):
    pix = lax.broadcasted_iota(jnp.int32, (128, 8), 0)
    lane = lax.broadcasted_iota(jnp.int32, (128, 8), 1)
    pick = (lax.rem(pix, 8) == lane).astype(F32)
    spread = jnp.dot(pick, mask.astype(F32), preferred_element_type=F32)
    place = lax.broadcasted_iota(jnp.int32, (128, 16), 0) // 8
    at = lax.broadcasted_iota(jnp.int32, (128, 16), 1)
    return jnp.sum(jnp.where(place == at, spread, 0.0), axis=1, keepdims=True)


def shifted(src, dst, start, rate, length, sign):
    wide = src.shape[1]
    for r in range(3):
        move = lax.rem(2 * wide - (start + sign * (r - 1) * rate), wide)
        dst[r] = pltpu.roll(src[...], move, 1)[:, :length].astype(BF)


def windows(src, start, rate, count, sign, rows=None):
    found = []
    for t in range(9):
        at = pl.ds(start + sign * (t % 3 - 1) * rate, count)
        piece = src[t // 3, at] if rows is None else src[t // 3, at, rows, :]
        found.append(piece.reshape(-1, 128))
    return jnp.concatenate(found, axis=1)


def kernel(
    pair_h, pmask_h, cmask_h, rates_h, wproj_h, wgate_h, wout_h, one_h, two_h, cot_h,
    output_ref, gpair_ref, total_ref,
    pair_v, pmask_v, cmask_v, rates_s, wproj_v, wgate_v, wout_v, one_v, two_v, in_sem,
    left, right, halves, first, cots, sums,
    field, taps, cfield, ctaps, hidden, htaps, gpre, gtaps, ghid,
    grads, parts, near, apart, final, partial,
    l_send, l_recv, l_recv2, l_far, r_send0, r_recv0, r_send, r_recv, r_relay,
    c_send, c_recv, c_send2, c_recv2, f_send, f_recv, f_send2, f_recv2,
    send1, recv1, send2, recv2, send3, recv3, send4, recv4, recv5,
):
    row = lax.axis_index("row")
    col = lax.axis_index("col")
    far = (col // 8) * 8 + (1 - lax.rem(col // 4, 2)) * 4 + lax.rem(col, 4)
    sibling = row + 1 - 2 * lax.rem(row, 2)
    turn_row = col // 2
    turn_col = 4 * lax.rem(row, 8)
    inward = jnp.where(lax.rem(col, 4) < 2, 1, -1)
    core = lax.rem(row, 2)
    z_hi = lax.rem(col // 4, 2)
    near_place = lax.rem(row // 2, 4)
    far_place = z_hi * 2 + row // 8
    me = core * 16 + plane_slot(col)

    def near_row(k):
        return (row // 8) * 8 + lax.rem(row + 2 * k, 8)

    def far_at(k):
        z = lax.rem(z_hi * 8 + row // 2 + 4 * k, 16)
        return lax.rem(z, 8) * 2 + core, (col // 8) * 8 + (z // 8) * 4 + lax.rem(col, 4)

    with jax.named_scope("start"):
        loads = [
            pltpu.make_async_copy(src, dst, in_sem.at[n])
            for n, (src, dst) in enumerate((
                (pair_h, pair_v), (pmask_h, pmask_v), (wproj_h, wproj_v), (cot_h, cots.at[7]),
                (wgate_h, wgate_v), (wout_h, wout_v), (cmask_h, cmask_v), (rates_h, rates_s),
                (two_h, two_v), (one_h, one_v),
            ))
        ]
        for load in loads:
            load.start()
        barrier = pltpu.get_barrier_semaphore()
        each(0, 16, lambda k: signal(barrier, sibling, plane_peer(col, k)))
        each(1, 16, lambda k: signal(barrier, row, plane_peer(col, k)))
        for k in range(1, 4):
            signal(barrier, near_row(k), col)
            signal(barrier, *far_at(k))
        beside = row + 2 * core - 1

        @pl.when((beside >= 0) & (beside < ROWS))
        def _():
            signal(barrier, beside, col)

        for shift in (1, 2, -1, -2):
            @pl.when(on_map(col + shift))
            def _():
                signal(barrier, row, col + shift)
        for n in range(4):
            @pl.when((turn_row != row) | (turn_col + n != col))
            def _():
                signal(barrier, turn_row, turn_col + n)

    with jax.named_scope("project"):
        for n in (0, 1, 2):
            loads[n].wait()
        pair = pair_v[...].astype(F32)
        normed = layer_norm(pair).astype(BF)
        projected = jnp.dot(normed, wproj_v[...], preferred_element_type=F32)
        mask = mask_column(pmask_v[...])
        left[col] = (mask * jax.nn.sigmoid(projected[:, 128:256]) * projected[:, :128]).astype(BF)
        halves[...] = (
            (mask * jax.nn.sigmoid(projected[:, 384:]) * projected[:, 256:384])
            .astype(BF)
            .reshape(2, 64, 128)
        )
        loads[3].wait()

    with jax.named_scope("barrier"):
        fixed = (turn_row == row) & (lax.rem(row, 8) == col // 4)
        pl.semaphore_wait(
            barrier,
            41
            - jnp.where(fixed, 1, 0)
            + jnp.where((beside >= 0) & (beside < ROWS), 1, 0)
            + jnp.minimum(col, 2)
            + jnp.minimum(COLS - 1 - col, 2),
        )

    def along_cols(buf, send_sem, recv_sem):
        for n, shift in enumerate(SHIFTS):
            @pl.when(on_map(col + shift))
            def _():
                remote(
                    buf.at[7], buf.at[7 - shift], send_sem.at[n], recv_sem.at[n], row, col + shift
                ).start()

            @pl.when(jnp.logical_not(on_map(col - shift)))
            def _():
                buf[7 - shift] = jnp.zeros((128, 128), BF)

    def wait_cols(buf, send_sem, recv_sem):
        for n, shift in enumerate(SHIFTS):
            @pl.when(on_map(col - shift))
            def _():
                wait_bytes(buf.at[7], recv_sem.at[n])
        for n, shift in enumerate(SHIFTS):
            @pl.when(on_map(col + shift))
            def _():
                wait_bytes(buf.at[7], send_sem.at[n])

    def along_rows(buf, send_sem, recv_sem):
        band = buf.at[pl.ds(5, 5)]
        none = jnp.zeros((5, 128, 128), BF)

        @pl.when(row < ROWS - 1)
        def _():
            remote(band, buf.at[pl.ds(0, 5)], send_sem.at[0], recv_sem.at[0], row + 1, col).start()

        @pl.when(row > 0)
        def _():
            remote(band, buf.at[pl.ds(10, 5)], send_sem.at[1], recv_sem.at[1], row - 1, col).start()

        @pl.when(row == 0)
        def _():
            buf[pl.ds(0, 5)] = none

        @pl.when(row == ROWS - 1)
        def _():
            buf[pl.ds(10, 5)] = none

    def wait_rows(buf, send_sem, recv_sem):
        @pl.when(row < ROWS - 1)
        def _():
            wait_bytes(buf.at[pl.ds(5, 5)], send_sem.at[0])
            wait_bytes(buf.at[pl.ds(10, 5)], recv_sem.at[1])

        @pl.when(row > 0)
        def _():
            wait_bytes(buf.at[pl.ds(5, 5)], send_sem.at[1])
            wait_bytes(buf.at[pl.ds(0, 5)], recv_sem.at[0])

    with jax.named_scope("turn"):
        def turn(half, low):
            return low * 8 + col // 4, 2 * row + half

        for half in range(2):
            for low in range(2):
                t_row, t_col = turn(half, low)

                @pl.when((t_row != row) | (t_col != col))
                def _():
                    remote(
                        halves.at[half], right.at[col], r_send0.at[2 * half + low],
                        r_recv0.at[lax.rem(col, 4)], t_row, t_col,
                    ).start()

                @pl.when((t_row == row) & (t_col == col))
                def _():
                    right[col] = halves[half]

        mine = left.at[col]
        remote(mine, mine, l_send, l_far, row, far).start()
        each(1, 16, lambda k: remote(mine, mine, l_send, l_recv, row, plane_peer(col, k)).start())

        for half in range(2):
            for low in range(2):
                t_row, t_col = turn(half, low)

                @pl.when((t_row != row) | (t_col != col))
                def _():
                    wait_bytes(halves.at[half], r_send0.at[2 * half + low])
        for n in range(4):
            @pl.when((turn_row != row) | (turn_col + n != col))
            def _():
                wait_bytes(right.at[0], r_recv0.at[n])

    with jax.named_scope("spread"):
        four = right.at[pl.ds(turn_col, 4)]
        each(1, 4, lambda k: remote(
            four, four, r_send, r_relay.at[lax.rem(row, 8) // 2],
            (row // 8) * 8 + lax.rem(row + 2 * k, 8), col).start())
        remote(four, four, r_send, r_recv, sibling, col).start()

    with jax.named_scope("farwait"):
        far_block = left.at[far]
        wait_bytes(far_block, l_far)
        each(1, 16, lambda k: remote(
            far_block, far_block, l_send, l_recv2, row, plane_peer(col, k)).start())

    along_cols(cots, c_send, c_recv)

    with jax.named_scope("relay"):
        def relay(k):
            p = lax.rem(row + ROWS - 2 * k, 8)
            block = right.at[pl.ds(4 * p, 4)]
            wait_bytes(block, r_relay.at[p // 2])
            remote(block, block, r_send, r_recv, sibling, col).start()

        each(1, 4, relay)
    with jax.named_scope("cotangent"):
        for n in range(4, 10):
            loads[n].wait()
        gating = jax.nn.sigmoid(jnp.dot(normed, wgate_v[...], preferred_element_type=F32))

    one_rate = rates_s[0]
    two_rate = rates_s[1]
    to = lax.broadcasted_iota(jnp.int32, (128, 128), 0)
    at = lax.broadcasted_iota(jnp.int32, (128, 128), 1)
    flip = ((lax.rem(to, 16) * 8 + to // 16) == at).astype(BF)
    flip_back = ((lax.rem(to, 8) * 16 + to // 8) == at).astype(BF)

    def unfold(src, dst, blocks):
        for n in blocks:
            dr, dc = n // 5 - 1, n % 5 - 2
            inside = (row + dr >= 0) & (row + dr < ROWS) & (col + dc >= 0) & (col + dc < COLS)
            cell = jnp.dot(flip, src[n], preferred_element_type=F32)
            dst[pl.ds((dc + 2) * 8, 8), pl.ds((dr + 1) * 16, 16), :] = jnp.where(
                inside, cell, 0.0
            ).reshape(8, 16, 128)

    def back(value):
        return jnp.dot(flip_back, value, preferred_element_type=F32).astype(BF)

    sibling_part = right.at[pl.ds(0, 16)]

    def add_from(half, part, total):
        def add(n, total):
            c = (n // 4) * 8 + half * 4 + lax.rem(n, 4)
            a = left[c, pl.ds(part * 32, 32), :].astype(F32).reshape(4, 1, 8, 128)
            b = right[c].astype(F32).reshape(1, 8, 8, 128)
            return total + a * b

        return lax.fori_loop(0, 16, add, total)

    with jax.named_scope("products"):
        @pl.when(core != z_hi)
        def _():
            wait_bytes(sibling_part, r_recv)

        wait_bytes(left.at[pl.ds(0, 15)], l_recv)
        for part in range(4):
            partial[part] = add_from(z_hi, part, jnp.zeros((4, 8, 8, 128), F32))
        wait_bytes(left.at[pl.ds(0, 15)], l_recv2)

        @pl.when(core == z_hi)
        def _():
            wait_bytes(sibling_part, r_recv)

        contact = mask_column(cmask_v[...])
        for half in range(2):
            for part in (2 * half, 2 * half + 1):
                total = add_from(1 - z_hi, part, partial[part])
                sums[pl.ds(part * 32, 32), :] = jnp.sum(total, axis=2).reshape(32, 128)
            rows = slice(64 * half, 64 * half + 64)
            product_norm = layer_norm(sums[rows, :]).astype(BF)
            new = (
                pair[rows]
                + gating[rows] * jnp.dot(product_norm, wout_v[...], preferred_element_type=F32)
            ).astype(BF).astype(F32)
            sums[rows, :] = new
            first[7, rows, :] = (layer_norm(new) * contact[rows]).astype(BF)
            for shift in (-inward, -2 * inward, inward, 2 * inward):
                @pl.when(on_map(col + shift))
                def _():
                    block = pl.ds(64 * half, 64)
                    remote(
                        first.at[7, block], first.at[7 - shift, block], f_send.at[2 + shift],
                        f_recv.at[2 - shift], row, col + shift,
                    ).start()

    with jax.named_scope("rimcols"):
        for shift in SHIFTS:
            @pl.when(jnp.logical_not(on_map(col - shift)))
            def _():
                first[7 - shift] = jnp.zeros((128, 128), BF)

        def hand_rows(delta):
            block = first.at[7 + delta]

            @pl.when(row < ROWS - 1)
            def _():
                remote(
                    block, first.at[2 + delta], f_send2.at[0], f_recv2.at[0, 2 + delta], row + 1, col
                ).start()

            @pl.when(row > 0)
            def _():
                remote(
                    block, first.at[12 + delta], f_send2.at[1], f_recv2.at[1, 2 + delta], row - 1, col
                ).start()

        def take_column(delta):
            @pl.when(on_map(col + delta))
            def _():
                wait_bytes(first.at[7], f_recv.at[2 + delta])

            hand_rows(delta)

        hand_rows(0)
        wait_cols(cots, c_send, c_recv)
        along_rows(cots, c_send2, c_recv2)
        take_column(inward)
        take_column(2 * inward)
        wait_rows(cots, c_send2, c_recv2)
    with jax.named_scope("hidden"):
        unfold(cots, cfield, range(15))
        shifted(cfield, ctaps, 8, two_rate, 32, -1)
        back_two = jnp.concatenate([two_v[t].T for t in range(9)], axis=0)
        ghid[...] = jnp.dot(
            windows(ctaps, 8, two_rate, 24, -1), back_two, preferred_element_type=F32
        )
    with jax.named_scope("rimwait"):
        take_column(-inward)
        take_column(-2 * inward)
        unfold(first, field, range(5, 10))
    with jax.named_scope("rimrows"):
        for shift in SHIFTS:
            @pl.when(on_map(col + shift))
            def _():
                wait_bytes(first.at[7], f_send.at[2 + shift])

        for delta in range(5):
            @pl.when(row < ROWS - 1)
            def _():
                wait_bytes(first.at[7], f_recv2.at[1, delta])

            @pl.when(row > 0)
            def _():
                wait_bytes(first.at[7], f_recv2.at[0, delta])

        @pl.when(row < ROWS - 1)
        def _():
            wait_bytes(first.at[pl.ds(0, 5)], f_send2.at[0])

        @pl.when(row > 0)
        def _():
            wait_bytes(first.at[pl.ds(0, 5)], f_send2.at[1])

    with jax.named_scope("unfold"):
        unfold(first, field, [*range(5), *range(10, 15)])
        shifted(field, taps, 8, one_rate, 32, 1)
    with jax.named_scope("conv"):
        pre = jnp.dot(
            windows(taps, 8, one_rate, 24, 1), one_v[...].reshape(1152, 128),
            preferred_element_type=F32,
        )
        c_at = lax.broadcasted_iota(jnp.int32, (24, 32, 128), 0) + (col * 8 - 8)
        r_at = lax.broadcasted_iota(jnp.int32, (24, 32, 128), 1) + (row * 16 - 8)
        inside = (c_at >= 0) & (c_at < 256) & (r_at >= 0) & (r_at < 256)
        sigma = jax.nn.sigmoid(pre)
        hidden[...] = jnp.where(inside, (pre * sigma).reshape(24, 32, 128), 0.0)
        gpre[...] = jnp.where(
            inside, (ghid[...] * sigma * (1.0 + pre * (1.0 - sigma))).reshape(24, 32, 128), 0.0
        )
        shifted(hidden, htaps, 8, two_rate, 16, 1)
    over = (((0,), (0,)), ((), ()))

    def scatter(there, chunk):
        def one(k):
            peer = plane_peer(col, k)

            @pl.when((k > 0) | (there != core))
            def _():
                remote(
                    grads.at[there * 16 + plane_slot(peer), CHUNKS[chunk]],
                    parts.at[me, CHUNKS[chunk]], send1, recv1.at[chunk],
                    row - core + there, peer,
                ).start()

        each(0, 16, one)

    def padded(value):
        return jnp.concatenate([value.astype(BF), jnp.zeros((128, 128), BF)]).reshape(16, 80, 128)

    with jax.named_scope("gradtwo"):
        cot_own = cots[7]
        second_taps = back(windows(htaps, 8, two_rate, 8, 1))
        grads[pl.ds(16, 16)] = padded(
            lax.dot_general(second_taps, cot_own, over, preferred_element_type=F32)
        )
        scatter(1, 0)
    with jax.named_scope("gradone"):
        gpre_own = gpre[pl.ds(8, 8), pl.ds(8, 16), :].reshape(128, 128).astype(BF)
        first_taps = windows(taps, 16, one_rate, 8, 1, pl.ds(8, 16))
        grads[pl.ds(0, 16)] = padded(
            lax.dot_general(first_taps, gpre_own, over, preferred_element_type=F32)
        )
        scatter(0, 0)
        scatter(1, 1)
        scatter(0, 1)
    with jax.named_scope("outputs"):
        parts[me] = grads[me]
        updated = sums[...]
        centre = updated - jnp.mean(updated, axis=-1, keepdims=True)
        inv = lax.rsqrt(jnp.mean(centre * centre, axis=-1, keepdims=True) + EPSILON)
        scaled = centre * inv
        second_pre = jnp.dot(
            second_taps, two_v[...].reshape(1152, 128), preferred_element_type=F32
        )
        output_ref[...] = (updated + second_pre).astype(BF)
        shifted(gpre, gtaps, 8, one_rate, 16, -1)
        back_one = jnp.concatenate([one_v[t].T for t in range(9)], axis=0)
        grad_in = contact * jnp.dot(
            back(windows(gtaps, 8, one_rate, 8, -1)), back_one, preferred_element_type=F32
        )
        grad_norm = inv * (
            grad_in
            - jnp.mean(grad_in, axis=-1, keepdims=True)
            - scaled * jnp.mean(grad_in * scaled, axis=-1, keepdims=True)
        )
        gpair_ref[...] = (cot_own.astype(F32) + grad_norm).astype(BF)

    def added(buf, count, chunk):
        total = buf[0, CHUNKS[chunk], :].astype(F32)
        for n in range(1, count):
            total = total + buf[n, CHUNKS[chunk], :].astype(F32)
        return total.astype(BF)

    most = parts.at[pl.ds(0, 31)]
    three = near.at[pl.ds(0, 3)]
    with jax.named_scope("near"):
        for chunk, rows in enumerate(CHUNKS):
            wait_bytes(parts.at[pl.ds(0, 31), rows], recv1.at[chunk])
            near[near_place, rows, :] = added(parts, 32, chunk)
            block = near.at[near_place, rows]
            for k in range(1, 4):
                remote(block, block, send2, recv2.at[chunk], near_row(k), col).start()
    with jax.named_scope("apart"):
        for chunk, rows in enumerate(CHUNKS):
            wait_bytes(near.at[pl.ds(0, 3), rows], recv2.at[chunk])
            apart[far_place, rows, :] = added(near, 4, chunk)
            block_far = apart.at[far_place, rows]
            for k in (2, 1, 3):
                remote(block_far, block_far, send3, recv3.at[chunk], *far_at(k)).start()
    with jax.named_scope("gather"):
        for chunk, rows in enumerate(CHUNKS):
            wait_bytes(apart.at[pl.ds(0, 3), rows], recv3.at[chunk])
            final[me, rows, :] = added(apart, 4, chunk)
            whole = final.at[me, rows]
            each(1, 16, lambda k: remote(
                whole, whole, send4, recv4.at[chunk, plane_slot(col)], row, plane_peer(col, k)
            ).start())
            remote(whole, whole, send4, recv5, sibling, col).start()

        for chunk, rows in enumerate(CHUNKS):
            def hand_on(k):
                slot = plane_slot(plane_peer(col, k))
                block = final.at[core * 16 + slot, rows]
                wait_bytes(block, recv4.at[chunk, slot])
                remote(block, block, send4, recv5, sibling, col).start()

            each(1, 16, hand_on)
        wait_bytes(right.at[pl.ds(0, 28)], r_send)
        wait_bytes(left.at[pl.ds(0, 31)], l_send)
        wait_bytes(most, send1)
        wait_bytes(three, send2)
        wait_bytes(three, send3)
        wait_bytes(final.at[pl.ds(0, 16)], recv5)
    with jax.named_scope("finish"):
        wait_bytes(most, send4)
        total_ref[...] = final[...]


def finish_kernel(output_in, gpair_in, total_in, output_ref, gpair_ref, one_ref, two_ref):
    output_ref[...] = output_in[...]
    gpair_ref[...] = gpair_in[...]
    for half, ref in enumerate((one_ref, two_ref)):
        grad = total_in[pl.ds(16 * half, 16)].reshape(1280, 128)[:1152].astype(F32)
        ref[...] = (grad * (1.0 / 256.0)).reshape(9, 128, 128)


VMEM = pltpu.VMEM
DMA = pltpu.SemaphoreType.DMA


def shape(dims, dtype):
    return jax.ShapeDtypeStruct(dims, dtype)


def local(
    pair, pair_mask, contact_mask, dilations, w_proj, w_gate, w_out, conv_one, conv_two, cotangent
):
    inputs = (
        pair.reshape(128, 128), pair_mask.T, contact_mask.T, dilations, w_proj, w_gate, w_out,
        conv_one, conv_two, cotangent.reshape(128, 128),
    )
    output, grad_pair, total = pl.pallas_call(
        kernel,
        out_shape=(shape((128, 128), BF), shape((128, 128), BF), shape((32, 80, 128), BF)),
        in_specs=[pl.BlockSpec(memory_space=pltpu.HBM)] * 10,
        out_specs=(pl.BlockSpec(memory_space=pltpu.VMEM),) * 3,
        scratch_shapes=[
            VMEM((128, 128), BF), VMEM((8, 16), jnp.int32), VMEM((8, 16), jnp.int32),
            pltpu.SMEM((2,), jnp.int32), VMEM((128, 512), BF), VMEM((128, 128), BF),
            VMEM((128, 128), BF), VMEM((9, 128, 128), BF), VMEM((9, 128, 128), BF), DMA((10,)),
            VMEM((32, 128, 128), BF), VMEM((32, 64, 128), BF), VMEM((2, 64, 128), BF),
            VMEM((15, 128, 128), BF), VMEM((15, 128, 128), BF), VMEM((128, 128), F32),
            VMEM((40, 48, 128), F32), VMEM((3, 40, 32, 128), BF),
            VMEM((40, 48, 128), F32), VMEM((3, 40, 32, 128), BF),
            VMEM((24, 32, 128), F32), VMEM((3, 24, 16, 128), BF),
            VMEM((24, 32, 128), F32), VMEM((3, 24, 16, 128), BF), VMEM((768, 128), F32),
            VMEM((32, 80, 128), BF), VMEM((32, 80, 128), BF), VMEM((4, 80, 128), BF),
            VMEM((4, 80, 128), BF), VMEM((32, 80, 128), BF), VMEM((4, 4, 8, 8, 128), F32),
            DMA, DMA, DMA, DMA, DMA((4,)), DMA((4,)), DMA, DMA, DMA((4,)),
            DMA((4,)), DMA((4,)), DMA((2,)), DMA((2,)),
            DMA((5,)), DMA((5,)), DMA((2,)), DMA((2, 5)),
            DMA, DMA((2,)), DMA, DMA((2,)), DMA, DMA((2,)), DMA, DMA((2, 16)), DMA,
        ],
        compiler_params=pltpu.CompilerParams(
            collective_id=1, has_side_effects=True, vmem_limit_bytes=62 << 20
        ),
    )(*inputs)
    whole = pl.BlockSpec(memory_space=pltpu.VMEM)
    output, grad_pair, grad_one, grad_two = pl.pallas_call(
        finish_kernel,
        out_shape=(
            shape((128, 128), BF), shape((128, 128), BF),
            shape((9, 128, 128), F32), shape((9, 128, 128), F32),
        ),
        in_specs=[whole] * 3,
        out_specs=(whole,) * 4,
    )(output, grad_pair, total)
    return (output.reshape(16, 8, 128), grad_pair.reshape(16, 8, 128), grad_one, grad_two)


def solution(mesh):
    in_specs = (
        P("row", "col", None), P("row", "col"), P("row", "col"), P(), P(), P(), P(), P(), P(),
        P("row", "col", None),
    )
    out_specs = (P("row", "col", None), P("row", "col", None), P(), P())
    return jax.shard_map(local, mesh=mesh, in_specs=in_specs, out_specs=out_specs, check_vma=False)
```

```python
import jax
import jax.numpy as jnp
from jax import lax
from jax.experimental import pallas as pl
from jax.experimental.pallas import tpu as pltpu
from jax.sharding import PartitionSpec as P

EPSILON = 1e-05
MESH = pl.DeviceIdType.MESH
BF = jnp.bfloat16
F32 = jnp.float32
ROWS = 16
COLS = 32
CHUNKS = (pl.ds(0, 48), pl.ds(48, 32))
SHIFTS = (1, 2, -1, -2)


def signal(sem, row, col):
    pl.semaphore_signal(sem, inc=1, device_id=(row, col), device_id_type=MESH)


def remote(src, dst, send_sem, recv_sem, row, col):
    return pltpu.make_async_remote_copy(
        src_ref=src,
        dst_ref=dst,
        send_sem=send_sem,
        recv_sem=recv_sem,
        device_id=(row, col),
        device_id_type=MESH,
    )


def wait_bytes(ref, sem):
    pltpu.make_async_copy(ref, ref, sem).wait()


def each(low, high, body):
    def step(k, carry):
        body(k)
        return carry

    lax.fori_loop(low, high, step, 0)


def plane_peer(col, k):
    x = lax.rem(col // 8 + k // 4, 4)
    y = lax.rem(lax.rem(col, 4) + lax.rem(k, 4), 4)
    return x * 8 + lax.rem(col // 4, 2) * 4 + y


def plane_slot(col):
    return (col // 8) * 4 + lax.rem(col, 4)


def on_map(col):
    return (col >= 0) & (col < COLS)


def layer_norm(values):
    centre = values - jnp.mean(values, axis=-1, keepdims=True)
    spread = jnp.mean(centre * centre, axis=-1, keepdims=True)
    return centre * lax.rsqrt(spread + EPSILON)


def mask_column(mask):
    pix = lax.broadcasted_iota(jnp.int32, (128, 8), 0)
    lane = lax.broadcasted_iota(jnp.int32, (128, 8), 1)
    pick = (lax.rem(pix, 8) == lane).astype(F32)
    spread = jnp.dot(pick, mask.astype(F32), preferred_element_type=F32)
    place = lax.broadcasted_iota(jnp.int32, (128, 16), 0) // 8
    at = lax.broadcasted_iota(jnp.int32, (128, 16), 1)
    return jnp.sum(jnp.where(place == at, spread, 0.0), axis=1, keepdims=True)


def shifted(src, dst, start, rate, length, sign):
    wide = src.shape[1]
    for r in range(3):
        move = lax.rem(2 * wide - (start + sign * (r - 1) * rate), wide)
        dst[r] = pltpu.roll(src[...], move, 1)[:, :length].astype(BF)


def windows(src, start, rate, count, sign, rows=None):
    found = []
    for t in range(9):
        at = pl.ds(start + sign * (t % 3 - 1) * rate, count)
        piece = src[t // 3, at] if rows is None else src[t // 3, at, rows, :]
        found.append(piece.reshape(-1, 128))
    return jnp.concatenate(found, axis=1)


def kernel(
    pair_h, pmask_h, cmask_h, rates_h, wproj_h, wgate_h, wout_h, one_h, two_h, cot_h,
    output_ref, gpair_ref, total_ref,
    pair_v, pmask_v, cmask_v, rates_s, wproj_v, wgate_v, wout_v, one_v, two_v, in_sem,
    left, right, halves, first, cots, sums,
    field, taps, cfield, ctaps, hidden, htaps, gpre, gtaps, ghid,
    grads, parts, near, apart, final, partial,
    l_send, l_recv, l_recv2, l_far, r_send0, r_recv0, r_send, r_recv, r_relay,
    c_send, c_recv, c_send2, c_recv2, f_send, f_recv, f_send2, f_recv2,
    send1, recv1, send2, recv2, send3, recv3, send4, recv4, recv5,
):
    row = lax.axis_index("row")
    col = lax.axis_index("col")
    far = (col // 8) * 8 + (1 - lax.rem(col // 4, 2)) * 4 + lax.rem(col, 4)
    sibling = row + 1 - 2 * lax.rem(row, 2)
    turn_row = col // 2
    turn_col = 4 * lax.rem(row, 8)
    inward = jnp.where(lax.rem(col, 4) < 2, 1, -1)
    core = lax.rem(row, 2)
    z_hi = lax.rem(col // 4, 2)
    near_place = lax.rem(row // 2, 4)
    far_place = z_hi * 2 + row // 8
    me = core * 16 + plane_slot(col)

    def near_row(k):
        return (row // 8) * 8 + lax.rem(row + 2 * k, 8)

    def far_at(k):
        z = lax.rem(z_hi * 8 + row // 2 + 4 * k, 16)
        return lax.rem(z, 8) * 2 + core, (col // 8) * 8 + (z // 8) * 4 + lax.rem(col, 4)

    with jax.named_scope("start"):
        barrier = pltpu.get_barrier_semaphore()
        for k in (2, 1, 3):
            signal(barrier, *far_at(k))
        for n in range(4):
            @pl.when((turn_row != row) | (turn_col + n != col))
            def _():
                signal(barrier, turn_row, turn_col + n)
        for shift in SHIFTS:
            @pl.when(on_map(col + shift))
            def _():
                signal(barrier, row, col + shift)
        for k in range(1, 4):
            signal(barrier, near_row(k), col)
        beside = row + 2 * core - 1

        @pl.when((beside >= 0) & (beside < ROWS))
        def _():
            signal(barrier, beside, col)

        each(1, 16, lambda k: signal(barrier, row, plane_peer(col, k)))
        each(0, 16, lambda k: signal(barrier, sibling, plane_peer(col, k)))

        loads = [
            pltpu.make_async_copy(src, dst, in_sem.at[n])
            for n, (src, dst) in enumerate((
                (pair_h, pair_v), (pmask_h, pmask_v), (wproj_h, wproj_v), (cot_h, cots.at[7]),
                (wgate_h, wgate_v), (wout_h, wout_v), (cmask_h, cmask_v), (rates_h, rates_s),
                (two_h, two_v), (one_h, one_v),
            ))
        ]
        for load in loads:
            load.start()
    with jax.named_scope("project"):
        for n in (0, 1, 2):
            loads[n].wait()
        pair = pair_v[...].astype(F32)
        normed = layer_norm(pair).astype(BF)
        projected = jnp.dot(normed, wproj_v[...], preferred_element_type=F32)
        mask = mask_column(pmask_v[...])
        left[col] = (mask * jax.nn.sigmoid(projected[:, 128:256]) * projected[:, :128]).astype(BF)
        halves[...] = (
            (mask * jax.nn.sigmoid(projected[:, 384:]) * projected[:, 256:384])
            .astype(BF)
            .reshape(2, 64, 128)
        )
        loads[3].wait()

    with jax.named_scope("barrier"):
        fixed = (turn_row == row) & (lax.rem(row, 8) == col // 4)
        pl.semaphore_wait(
            barrier,
            41
            - jnp.where(fixed, 1, 0)
            + jnp.where((beside >= 0) & (beside < ROWS), 1, 0)
            + jnp.minimum(col, 2)
            + jnp.minimum(COLS - 1 - col, 2),
        )

    def along_cols(buf, send_sem, recv_sem):
        for n, shift in enumerate(SHIFTS):
            @pl.when(on_map(col + shift))
            def _():
                remote(
                    buf.at[7], buf.at[7 - shift], send_sem.at[n], recv_sem.at[n], row, col + shift
                ).start()

            @pl.when(jnp.logical_not(on_map(col - shift)))
            def _():
                buf[7 - shift] = jnp.zeros((128, 128), BF)

    def wait_cols(buf, send_sem, recv_sem):
        for n, shift in enumerate(SHIFTS):
            @pl.when(on_map(col - shift))
            def _():
                wait_bytes(buf.at[7], recv_sem.at[n])
        for n, shift in enumerate(SHIFTS):
            @pl.when(on_map(col + shift))
            def _():
                wait_bytes(buf.at[7], send_sem.at[n])

    def along_rows(buf, send_sem, recv_sem):
        band = buf.at[pl.ds(5, 5)]
        none = jnp.zeros((5, 128, 128), BF)

        @pl.when(row < ROWS - 1)
        def _():
            remote(band, buf.at[pl.ds(0, 5)], send_sem.at[0], recv_sem.at[0], row + 1, col).start()

        @pl.when(row > 0)
        def _():
            remote(band, buf.at[pl.ds(10, 5)], send_sem.at[1], recv_sem.at[1], row - 1, col).start()

        @pl.when(row == 0)
        def _():
            buf[pl.ds(0, 5)] = none

        @pl.when(row == ROWS - 1)
        def _():
            buf[pl.ds(10, 5)] = none

    def wait_rows(buf, send_sem, recv_sem):
        @pl.when(row < ROWS - 1)
        def _():
            wait_bytes(buf.at[pl.ds(5, 5)], send_sem.at[0])
            wait_bytes(buf.at[pl.ds(10, 5)], recv_sem.at[1])

        @pl.when(row > 0)
        def _():
            wait_bytes(buf.at[pl.ds(5, 5)], send_sem.at[1])
            wait_bytes(buf.at[pl.ds(0, 5)], recv_sem.at[0])

    with jax.named_scope("turn"):
        def turn(half, low):
            return low * 8 + col // 4, 2 * row + half

        for half in range(2):
            for low in range(2):
                t_row, t_col = turn(half, low)

                @pl.when((t_row != row) | (t_col != col))
                def _():
                    remote(
                        halves.at[half], right.at[col], r_send0.at[2 * half + low],
                        r_recv0.at[lax.rem(col, 4)], t_row, t_col,
                    ).start()

                @pl.when((t_row == row) & (t_col == col))
                def _():
                    right[col] = halves[half]

        mine = left.at[col]
        remote(mine, mine, l_send, l_far, row, far).start()
        each(1, 16, lambda k: remote(mine, mine, l_send, l_recv, row, plane_peer(col, k)).start())

        for half in range(2):
            for low in range(2):
                t_row, t_col = turn(half, low)

                @pl.when((t_row != row) | (t_col != col))
                def _():
                    wait_bytes(halves.at[half], r_send0.at[2 * half + low])
        for n in range(4):
            @pl.when((turn_row != row) | (turn_col + n != col))
            def _():
                wait_bytes(right.at[0], r_recv0.at[n])

    with jax.named_scope("spread"):
        four = right.at[pl.ds(turn_col, 4)]
        each(1, 4, lambda k: remote(
            four, four, r_send, r_relay.at[lax.rem(row, 8) // 2],
            (row // 8) * 8 + lax.rem(row + 2 * k, 8), col).start())
        remote(four, four, r_send, r_recv, sibling, col).start()

    with jax.named_scope("farwait"):
        far_block = left.at[far]
        wait_bytes(far_block, l_far)
        each(1, 16, lambda k: remote(
            far_block, far_block, l_send, l_recv2, row, plane_peer(col, k)).start())

    with jax.named_scope("relay"):
        def relay(k):
            p = lax.rem(row + ROWS - 2 * k, 8)
            block = right.at[pl.ds(4 * p, 4)]
            wait_bytes(block, r_relay.at[p // 2])
            remote(block, block, r_send, r_recv, sibling, col).start()

        each(1, 4, relay)
    along_cols(cots, c_send, c_recv)

    with jax.named_scope("cotangent"):
        for n in range(4, 10):
            loads[n].wait()
        gating = jax.nn.sigmoid(jnp.dot(normed, wgate_v[...], preferred_element_type=F32))

    one_rate = rates_s[0]
    two_rate = rates_s[1]
    to = lax.broadcasted_iota(jnp.int32, (128, 128), 0)
    at = lax.broadcasted_iota(jnp.int32, (128, 128), 1)
    flip = ((lax.rem(to, 16) * 8 + to // 16) == at).astype(BF)
    flip_back = ((lax.rem(to, 8) * 16 + to // 8) == at).astype(BF)

    def unfold(src, dst, blocks):
        for n in blocks:
            dr, dc = n // 5 - 1, n % 5 - 2
            inside = (row + dr >= 0) & (row + dr < ROWS) & (col + dc >= 0) & (col + dc < COLS)
            cell = jnp.dot(flip, src[n], preferred_element_type=F32)
            dst[pl.ds((dc + 2) * 8, 8), pl.ds((dr + 1) * 16, 16), :] = jnp.where(
                inside, cell, 0.0
            ).reshape(8, 16, 128)

    def back(value):
        return jnp.dot(flip_back, value, preferred_element_type=F32).astype(BF)

    sibling_part = right.at[pl.ds(0, 16)]

    def add_from(half, part, total):
        def add(n, total):
            c = (n // 4) * 8 + half * 4 + lax.rem(n, 4)
            a = left[c, pl.ds(part * 32, 32), :].astype(F32).reshape(4, 1, 8, 128)
            b = right[c].astype(F32).reshape(1, 8, 8, 128)
            return total + a * b

        return lax.fori_loop(0, 16, add, total)

    with jax.named_scope("products"):
        @pl.when(core != z_hi)
        def _():
            wait_bytes(sibling_part, r_recv)

        wait_bytes(left.at[pl.ds(0, 15)], l_recv)
        for part in range(4):
            partial[part] = add_from(z_hi, part, jnp.zeros((4, 8, 8, 128), F32))
        wait_bytes(left.at[pl.ds(0, 15)], l_recv2)

        @pl.when(core == z_hi)
        def _():
            wait_bytes(sibling_part, r_recv)

        contact = mask_column(cmask_v[...])
        for half in range(2):
            for part in (2 * half, 2 * half + 1):
                total = add_from(1 - z_hi, part, partial[part])
                sums[pl.ds(part * 32, 32), :] = jnp.sum(total, axis=2).reshape(32, 128)
            rows = slice(64 * half, 64 * half + 64)
            product_norm = layer_norm(sums[rows, :]).astype(BF)
            new = (
                pair[rows]
                + gating[rows] * jnp.dot(product_norm, wout_v[...], preferred_element_type=F32)
            ).astype(BF).astype(F32)
            sums[rows, :] = new
            first[7, rows, :] = (layer_norm(new) * contact[rows]).astype(BF)
            for shift in (-inward, -2 * inward, inward, 2 * inward):
                @pl.when(on_map(col + shift))
                def _():
                    block = pl.ds(64 * half, 64)
                    remote(
                        first.at[7, block], first.at[7 - shift, block], f_send.at[2 + shift],
                        f_recv.at[2 - shift], row, col + shift,
                    ).start()

    with jax.named_scope("rimcols"):
        for shift in SHIFTS:
            @pl.when(jnp.logical_not(on_map(col - shift)))
            def _():
                first[7 - shift] = jnp.zeros((128, 128), BF)

        def hand_rows(delta):
            block = first.at[7 + delta]

            @pl.when(row < ROWS - 1)
            def _():
                remote(
                    block, first.at[2 + delta], f_send2.at[0], f_recv2.at[0, 2 + delta], row + 1, col
                ).start()

            @pl.when(row > 0)
            def _():
                remote(
                    block, first.at[12 + delta], f_send2.at[1], f_recv2.at[1, 2 + delta], row - 1, col
                ).start()

        def take_column(delta):
            @pl.when(on_map(col + delta))
            def _():
                wait_bytes(first.at[7], f_recv.at[2 + delta])

            hand_rows(delta)

        hand_rows(0)
        wait_cols(cots, c_send, c_recv)
        along_rows(cots, c_send2, c_recv2)
        take_column(inward)
        take_column(2 * inward)
        wait_rows(cots, c_send2, c_recv2)
    with jax.named_scope("hidden"):
        unfold(cots, cfield, range(15))
        shifted(cfield, ctaps, 8, two_rate, 32, -1)
        back_two = jnp.concatenate([two_v[t].T for t in range(9)], axis=0)
        ghid[...] = jnp.dot(
            windows(ctaps, 8, two_rate, 24, -1), back_two, preferred_element_type=F32
        )
    with jax.named_scope("rimwait"):
        take_column(-inward)
        take_column(-2 * inward)
        unfold(first, field, range(5, 10))
    with jax.named_scope("rimrows"):
        for shift in SHIFTS:
            @pl.when(on_map(col + shift))
            def _():
                wait_bytes(first.at[7], f_send.at[2 + shift])

        for delta in range(5):
            @pl.when(row < ROWS - 1)
            def _():
                wait_bytes(first.at[7], f_recv2.at[1, delta])

            @pl.when(row > 0)
            def _():
                wait_bytes(first.at[7], f_recv2.at[0, delta])

        @pl.when(row < ROWS - 1)
        def _():
            wait_bytes(first.at[pl.ds(0, 5)], f_send2.at[0])

        @pl.when(row > 0)
        def _():
            wait_bytes(first.at[pl.ds(0, 5)], f_send2.at[1])

    with jax.named_scope("unfold"):
        unfold(first, field, [*range(5), *range(10, 15)])
        shifted(field, taps, 8, one_rate, 32, 1)
    with jax.named_scope("conv"):
        pre = jnp.dot(
            windows(taps, 8, one_rate, 24, 1), one_v[...].reshape(1152, 128),
            preferred_element_type=F32,
        )
        c_at = lax.broadcasted_iota(jnp.int32, (24, 32, 128), 0) + (col * 8 - 8)
        r_at = lax.broadcasted_iota(jnp.int32, (24, 32, 128), 1) + (row * 16 - 8)
        inside = (c_at >= 0) & (c_at < 256) & (r_at >= 0) & (r_at < 256)
        sigma = jax.nn.sigmoid(pre)
        hidden[...] = jnp.where(inside, (pre * sigma).reshape(24, 32, 128), 0.0)
        gpre[...] = jnp.where(
            inside, (ghid[...] * sigma * (1.0 + pre * (1.0 - sigma))).reshape(24, 32, 128), 0.0
        )
        shifted(hidden, htaps, 8, two_rate, 16, 1)
    over = (((0,), (0,)), ((), ()))

    def scatter(there, chunk):
        def one(k):
            peer = plane_peer(col, k)

            @pl.when((k > 0) | (there != core))
            def _():
                remote(
                    grads.at[there * 16 + plane_slot(peer), CHUNKS[chunk]],
                    parts.at[me, CHUNKS[chunk]], send1, recv1.at[chunk],
                    row - core + there, peer,
                ).start()

        each(0, 16, one)

    def padded(value):
        return jnp.concatenate([value.astype(BF), jnp.zeros((128, 128), BF)]).reshape(16, 80, 128)

    with jax.named_scope("gradtwo"):
        cot_own = cots[7]
        second_taps = back(windows(htaps, 8, two_rate, 8, 1))
        grads[pl.ds(16, 16)] = padded(
            lax.dot_general(second_taps, cot_own, over, preferred_element_type=F32)
        )
        scatter(1, 0)
    with jax.named_scope("gradone"):
        gpre_own = gpre[pl.ds(8, 8), pl.ds(8, 16), :].reshape(128, 128).astype(BF)
        first_taps = windows(taps, 16, one_rate, 8, 1, pl.ds(8, 16))
        grads[pl.ds(0, 16)] = padded(
            lax.dot_general(first_taps, gpre_own, over, preferred_element_type=F32)
        )
        scatter(0, 0)
        scatter(1, 1)
        scatter(0, 1)
    with jax.named_scope("outputs"):
        parts[me] = grads[me]
        updated = sums[...]
        centre = updated - jnp.mean(updated, axis=-1, keepdims=True)
        inv = lax.rsqrt(jnp.mean(centre * centre, axis=-1, keepdims=True) + EPSILON)
        scaled = centre * inv
        second_pre = jnp.dot(
            second_taps, two_v[...].reshape(1152, 128), preferred_element_type=F32
        )
        output_ref[...] = (updated + second_pre).astype(BF)
        shifted(gpre, gtaps, 8, one_rate, 16, -1)
        back_one = jnp.concatenate([one_v[t].T for t in range(9)], axis=0)
        grad_in = contact * jnp.dot(
            back(windows(gtaps, 8, one_rate, 8, -1)), back_one, preferred_element_type=F32
        )
        grad_norm = inv * (
            grad_in
            - jnp.mean(grad_in, axis=-1, keepdims=True)
            - scaled * jnp.mean(grad_in * scaled, axis=-1, keepdims=True)
        )
        gpair_ref[...] = (cot_own.astype(F32) + grad_norm).astype(BF)

    def added(buf, count, chunk):
        total = buf[0, CHUNKS[chunk], :].astype(F32)
        for n in range(1, count):
            total = total + buf[n, CHUNKS[chunk], :].astype(F32)
        return total.astype(BF)

    most = parts.at[pl.ds(0, 31)]
    three = near.at[pl.ds(0, 3)]
    with jax.named_scope("near"):
        for chunk, rows in enumerate(CHUNKS):
            wait_bytes(parts.at[pl.ds(0, 31), rows], recv1.at[chunk])
            near[near_place, rows, :] = added(parts, 32, chunk)
            block = near.at[near_place, rows]
            for k in range(1, 4):
                remote(block, block, send2, recv2.at[chunk], near_row(k), col).start()
    with jax.named_scope("apart"):
        for chunk, rows in enumerate(CHUNKS):
            wait_bytes(near.at[pl.ds(0, 3), rows], recv2.at[chunk])
            apart[far_place, rows, :] = added(near, 4, chunk)
            block_far = apart.at[far_place, rows]
            for k in (2, 1, 3):
                remote(block_far, block_far, send3, recv3.at[chunk], *far_at(k)).start()
    with jax.named_scope("gather"):
        for chunk, rows in enumerate(CHUNKS):
            wait_bytes(apart.at[pl.ds(0, 3), rows], recv3.at[chunk])
            final[me, rows, :] = added(apart, 4, chunk)
            whole = final.at[me, rows]
            each(1, 16, lambda k: remote(
                whole, whole, send4, recv4.at[chunk, plane_slot(col)], row, plane_peer(col, k)
            ).start())
            remote(whole, whole, send4, recv5, sibling, col).start()

        for chunk, rows in enumerate(CHUNKS):
            def hand_on(k):
                slot = plane_slot(plane_peer(col, k))
                block = final.at[core * 16 + slot, rows]
                wait_bytes(block, recv4.at[chunk, slot])
                remote(block, block, send4, recv5, sibling, col).start()

            each(1, 16, hand_on)
        wait_bytes(right.at[pl.ds(0, 28)], r_send)
        wait_bytes(left.at[pl.ds(0, 31)], l_send)
        wait_bytes(most, send1)
        wait_bytes(three, send2)
        wait_bytes(three, send3)
        wait_bytes(final.at[pl.ds(0, 16)], recv5)
    with jax.named_scope("finish"):
        wait_bytes(most, send4)
        total_ref[...] = final[...]


def finish_kernel(output_in, gpair_in, total_in, output_ref, gpair_ref, one_ref, two_ref):
    output_ref[...] = output_in[...]
    gpair_ref[...] = gpair_in[...]
    for half, ref in enumerate((one_ref, two_ref)):
        grad = total_in[pl.ds(16 * half, 16)].reshape(1280, 128)[:1152].astype(F32)
        ref[...] = (grad * (1.0 / 256.0)).reshape(9, 128, 128)


VMEM = pltpu.VMEM
DMA = pltpu.SemaphoreType.DMA


def shape(dims, dtype):
    return jax.ShapeDtypeStruct(dims, dtype)


def local(
    pair, pair_mask, contact_mask, dilations, w_proj, w_gate, w_out, conv_one, conv_two, cotangent
):
    inputs = (
        pair.reshape(128, 128), pair_mask.T, contact_mask.T, dilations, w_proj, w_gate, w_out,
        conv_one, conv_two, cotangent.reshape(128, 128),
    )
    output, grad_pair, total = pl.pallas_call(
        kernel,
        out_shape=(shape((128, 128), BF), shape((128, 128), BF), shape((32, 80, 128), BF)),
        in_specs=[pl.BlockSpec(memory_space=pltpu.HBM)] * 10,
        out_specs=(pl.BlockSpec(memory_space=pltpu.VMEM),) * 3,
        scratch_shapes=[
            VMEM((128, 128), BF), VMEM((8, 16), jnp.int32), VMEM((8, 16), jnp.int32),
            pltpu.SMEM((2,), jnp.int32), VMEM((128, 512), BF), VMEM((128, 128), BF),
            VMEM((128, 128), BF), VMEM((9, 128, 128), BF), VMEM((9, 128, 128), BF), DMA((10,)),
            VMEM((32, 128, 128), BF), VMEM((32, 64, 128), BF), VMEM((2, 64, 128), BF),
            VMEM((15, 128, 128), BF), VMEM((15, 128, 128), BF), VMEM((128, 128), F32),
            VMEM((40, 48, 128), F32), VMEM((3, 40, 32, 128), BF),
            VMEM((40, 48, 128), F32), VMEM((3, 40, 32, 128), BF),
            VMEM((24, 32, 128), F32), VMEM((3, 24, 16, 128), BF),
            VMEM((24, 32, 128), F32), VMEM((3, 24, 16, 128), BF), VMEM((768, 128), F32),
            VMEM((32, 80, 128), BF), VMEM((32, 80, 128), BF), VMEM((4, 80, 128), BF),
            VMEM((4, 80, 128), BF), VMEM((32, 80, 128), BF), VMEM((4, 4, 8, 8, 128), F32),
            DMA, DMA, DMA, DMA, DMA((4,)), DMA((4,)), DMA, DMA, DMA((4,)),
            DMA((4,)), DMA((4,)), DMA((2,)), DMA((2,)),
            DMA((5,)), DMA((5,)), DMA((2,)), DMA((2, 5)),
            DMA, DMA((2,)), DMA, DMA((2,)), DMA, DMA((2,)), DMA, DMA((2, 16)), DMA,
        ],
        compiler_params=pltpu.CompilerParams(
            collective_id=1, has_side_effects=True, vmem_limit_bytes=62 << 20
        ),
    )(*inputs)
    whole = pl.BlockSpec(memory_space=pltpu.VMEM)
    output, grad_pair, grad_one, grad_two = pl.pallas_call(
        finish_kernel,
        out_shape=(
            shape((128, 128), BF), shape((128, 128), BF),
            shape((9, 128, 128), F32), shape((9, 128, 128), F32),
        ),
        in_specs=[whole] * 3,
        out_specs=(whole,) * 4,
    )(output, grad_pair, total)
    return (output.reshape(16, 8, 128), grad_pair.reshape(16, 8, 128), grad_one, grad_two)


def solution(mesh):
    in_specs = (
        P("row", "col", None), P("row", "col"), P("row", "col"), P(), P(), P(), P(), P(), P(),
        P("row", "col", None),
    )
    out_specs = (P("row", "col", None), P("row", "col", None), P(), P())
    return jax.shard_map(local, mesh=mesh, in_specs=in_specs, out_specs=out_specs, check_vma=False)
```

```python
import jax
import jax.numpy as jnp
from jax import lax
from jax.experimental import pallas as pl
from jax.experimental.pallas import tpu as pltpu
from jax.sharding import PartitionSpec as P

EPSILON = 1e-05
MESH = pl.DeviceIdType.MESH
BF = jnp.bfloat16
F32 = jnp.float32
ROWS = 16
COLS = 32
CHUNKS = (pl.ds(0, 48), pl.ds(48, 32))
SHIFTS = (1, 2, -1, -2)


def signal(sem, row, col):
    pl.semaphore_signal(sem, inc=1, device_id=(row, col), device_id_type=MESH)


def remote(src, dst, send_sem, recv_sem, row, col):
    return pltpu.make_async_remote_copy(
        src_ref=src,
        dst_ref=dst,
        send_sem=send_sem,
        recv_sem=recv_sem,
        device_id=(row, col),
        device_id_type=MESH,
    )


def wait_bytes(ref, sem):
    pltpu.make_async_copy(ref, ref, sem).wait()


def each(low, high, body):
    def step(k, carry):
        body(k)
        return carry

    lax.fori_loop(low, high, step, 0)


def plane_peer(col, k):
    x = lax.rem(col // 8 + k // 4, 4)
    y = lax.rem(lax.rem(col, 4) + lax.rem(k, 4), 4)
    return x * 8 + lax.rem(col // 4, 2) * 4 + y


def plane_slot(col):
    return (col // 8) * 4 + lax.rem(col, 4)


def on_map(col):
    return (col >= 0) & (col < COLS)


def layer_norm(values):
    centre = values - jnp.mean(values, axis=-1, keepdims=True)
    spread = jnp.mean(centre * centre, axis=-1, keepdims=True)
    return centre * lax.rsqrt(spread + EPSILON)


def mask_column(mask):
    pix = lax.broadcasted_iota(jnp.int32, (128, 8), 0)
    lane = lax.broadcasted_iota(jnp.int32, (128, 8), 1)
    pick = (lax.rem(pix, 8) == lane).astype(F32)
    spread = jnp.dot(pick, mask.astype(F32), preferred_element_type=F32)
    place = lax.broadcasted_iota(jnp.int32, (128, 16), 0) // 8
    at = lax.broadcasted_iota(jnp.int32, (128, 16), 1)
    return jnp.sum(jnp.where(place == at, spread, 0.0), axis=1, keepdims=True)


def shifted(src, dst, start, rate, length, sign):
    wide = src.shape[1]
    for r in range(3):
        move = lax.rem(2 * wide - (start + sign * (r - 1) * rate), wide)
        dst[r] = pltpu.roll(src[...], move, 1)[:, :length].astype(BF)


def windows(src, start, rate, count, sign, rows=None):
    found = []
    for t in range(9):
        at = pl.ds(start + sign * (t % 3 - 1) * rate, count)
        piece = src[t // 3, at] if rows is None else src[t // 3, at, rows, :]
        found.append(piece.reshape(-1, 128))
    return jnp.concatenate(found, axis=1)


def kernel(
    pair_h, pmask_h, cmask_h, rates_h, wproj_h, wgate_h, wout_h, one_h, two_h, cot_h,
    output_ref, gpair_ref, total_ref,
    pair_v, pmask_v, cmask_v, rates_s, wproj_v, wgate_v, wout_v, one_v, two_v, in_sem,
    left, right, halves, first, cots, sums,
    field, taps, cfield, ctaps, hidden, htaps, gpre, gtaps, ghid,
    grads, parts, near, apart, final, partial,
    l_send, l_recv, l_recv2, l_far, r_send0, r_recv0, r_send, r_recv, r_relay,
    c_send, c_recv, c_send2, c_recv2, f_send, f_recv, f_send2, f_recv2,
    send1, recv1, send2, recv2, send3, recv3, send4, recv4, recv5,
):
    row = lax.axis_index("row")
    col = lax.axis_index("col")
    far = (col // 8) * 8 + (1 - lax.rem(col // 4, 2)) * 4 + lax.rem(col, 4)
    sibling = row + 1 - 2 * lax.rem(row, 2)
    turn_row = col // 2
    turn_col = 4 * lax.rem(row, 8)
    inward = jnp.where(lax.rem(col, 4) < 2, 1, -1)
    core = lax.rem(row, 2)
    z_hi = lax.rem(col // 4, 2)
    near_place = lax.rem(row // 2, 4)
    far_place = z_hi * 2 + row // 8
    me = core * 16 + plane_slot(col)

    def near_row(k):
        return (row // 8) * 8 + lax.rem(row + 2 * k, 8)

    def far_at(k):
        z = lax.rem(z_hi * 8 + row // 2 + 4 * k, 16)
        return lax.rem(z, 8) * 2 + core, (col // 8) * 8 + (z // 8) * 4 + lax.rem(col, 4)

    if True:
        barrier = pltpu.get_barrier_semaphore()
        for k in (2, 1, 3):
            signal(barrier, *far_at(k))
        for n in range(4):
            @pl.when((turn_row != row) | (turn_col + n != col))
            def _():
                signal(barrier, turn_row, turn_col + n)
        for shift in SHIFTS:
            @pl.when(on_map(col + shift))
            def _():
                signal(barrier, row, col + shift)
        for k in range(1, 4):
            signal(barrier, near_row(k), col)
        beside = row + 2 * core - 1

        @pl.when((beside >= 0) & (beside < ROWS))
        def _():
            signal(barrier, beside, col)

        each(1, 16, lambda k: signal(barrier, row, plane_peer(col, k)))
        each(0, 16, lambda k: signal(barrier, sibling, plane_peer(col, k)))

        loads = [
            pltpu.make_async_copy(src, dst, in_sem.at[n])
            for n, (src, dst) in enumerate((
                (pair_h, pair_v), (pmask_h, pmask_v), (wproj_h, wproj_v), (cot_h, cots.at[7]),
                (wgate_h, wgate_v), (wout_h, wout_v), (cmask_h, cmask_v), (rates_h, rates_s),
                (two_h, two_v), (one_h, one_v),
            ))
        ]
        for load in loads:
            load.start()
    if True:
        for n in (0, 1, 2):
            loads[n].wait()
        pair = pair_v[...].astype(F32)
        normed = layer_norm(pair).astype(BF)
        projected = jnp.dot(normed, wproj_v[...], preferred_element_type=F32)
        mask = mask_column(pmask_v[...])
        left[col] = (mask * jax.nn.sigmoid(projected[:, 128:256]) * projected[:, :128]).astype(BF)
        halves[...] = (
            (mask * jax.nn.sigmoid(projected[:, 384:]) * projected[:, 256:384])
            .astype(BF)
            .reshape(2, 64, 128)
        )
        loads[3].wait()

    if True:
        fixed = (turn_row == row) & (lax.rem(row, 8) == col // 4)
        pl.semaphore_wait(
            barrier,
            41
            - jnp.where(fixed, 1, 0)
            + jnp.where((beside >= 0) & (beside < ROWS), 1, 0)
            + jnp.minimum(col, 2)
            + jnp.minimum(COLS - 1 - col, 2),
        )

    def along_cols(buf, send_sem, recv_sem):
        for n, shift in enumerate(SHIFTS):
            @pl.when(on_map(col + shift))
            def _():
                remote(
                    buf.at[7], buf.at[7 - shift], send_sem.at[n], recv_sem.at[n], row, col + shift
                ).start()

            @pl.when(jnp.logical_not(on_map(col - shift)))
            def _():
                buf[7 - shift] = jnp.zeros((128, 128), BF)

    def wait_cols(buf, send_sem, recv_sem):
        for n, shift in enumerate(SHIFTS):
            @pl.when(on_map(col - shift))
            def _():
                wait_bytes(buf.at[7], recv_sem.at[n])
        for n, shift in enumerate(SHIFTS):
            @pl.when(on_map(col + shift))
            def _():
                wait_bytes(buf.at[7], send_sem.at[n])

    def along_rows(buf, send_sem, recv_sem):
        band = buf.at[pl.ds(5, 5)]
        none = jnp.zeros((5, 128, 128), BF)

        @pl.when(row < ROWS - 1)
        def _():
            remote(band, buf.at[pl.ds(0, 5)], send_sem.at[0], recv_sem.at[0], row + 1, col).start()

        @pl.when(row > 0)
        def _():
            remote(band, buf.at[pl.ds(10, 5)], send_sem.at[1], recv_sem.at[1], row - 1, col).start()

        @pl.when(row == 0)
        def _():
            buf[pl.ds(0, 5)] = none

        @pl.when(row == ROWS - 1)
        def _():
            buf[pl.ds(10, 5)] = none

    def wait_rows(buf, send_sem, recv_sem):
        @pl.when(row < ROWS - 1)
        def _():
            wait_bytes(buf.at[pl.ds(5, 5)], send_sem.at[0])
            wait_bytes(buf.at[pl.ds(10, 5)], recv_sem.at[1])

        @pl.when(row > 0)
        def _():
            wait_bytes(buf.at[pl.ds(5, 5)], send_sem.at[1])
            wait_bytes(buf.at[pl.ds(0, 5)], recv_sem.at[0])

    if True:
        def turn(half, low):
            return low * 8 + col // 4, 2 * row + half

        for half in range(2):
            for low in range(2):
                t_row, t_col = turn(half, low)

                @pl.when((t_row != row) | (t_col != col))
                def _():
                    remote(
                        halves.at[half], right.at[col], r_send0.at[2 * half + low],
                        r_recv0.at[lax.rem(col, 4)], t_row, t_col,
                    ).start()

                @pl.when((t_row == row) & (t_col == col))
                def _():
                    right[col] = halves[half]

        mine = left.at[col]
        remote(mine, mine, l_send, l_far, row, far).start()
        each(1, 16, lambda k: remote(mine, mine, l_send, l_recv, row, plane_peer(col, k)).start())

        for half in range(2):
            for low in range(2):
                t_row, t_col = turn(half, low)

                @pl.when((t_row != row) | (t_col != col))
                def _():
                    wait_bytes(halves.at[half], r_send0.at[2 * half + low])
        for n in range(4):
            @pl.when((turn_row != row) | (turn_col + n != col))
            def _():
                wait_bytes(right.at[0], r_recv0.at[n])

    if True:
        four = right.at[pl.ds(turn_col, 4)]
        each(1, 4, lambda k: remote(
            four, four, r_send, r_relay.at[lax.rem(row, 8) // 2],
            (row // 8) * 8 + lax.rem(row + 2 * k, 8), col).start())
        remote(four, four, r_send, r_recv, sibling, col).start()

    if True:
        far_block = left.at[far]
        wait_bytes(far_block, l_far)
        each(1, 16, lambda k: remote(
            far_block, far_block, l_send, l_recv2, row, plane_peer(col, k)).start())

    if True:
        def relay(k):
            p = lax.rem(row + ROWS - 2 * k, 8)
            block = right.at[pl.ds(4 * p, 4)]
            wait_bytes(block, r_relay.at[p // 2])
            remote(block, block, r_send, r_recv, sibling, col).start()

        each(1, 4, relay)
    along_cols(cots, c_send, c_recv)

    if True:
        for n in range(4, 10):
            loads[n].wait()
        gating = jax.nn.sigmoid(jnp.dot(normed, wgate_v[...], preferred_element_type=F32))

    one_rate = rates_s[0]
    two_rate = rates_s[1]
    to = lax.broadcasted_iota(jnp.int32, (128, 128), 0)
    at = lax.broadcasted_iota(jnp.int32, (128, 128), 1)
    flip = ((lax.rem(to, 16) * 8 + to // 16) == at).astype(BF)
    flip_back = ((lax.rem(to, 8) * 16 + to // 8) == at).astype(BF)

    def unfold(src, dst, blocks):
        for n in blocks:
            dr, dc = n // 5 - 1, n % 5 - 2
            inside = (row + dr >= 0) & (row + dr < ROWS) & (col + dc >= 0) & (col + dc < COLS)
            cell = jnp.dot(flip, src[n], preferred_element_type=F32)
            dst[pl.ds((dc + 2) * 8, 8), pl.ds((dr + 1) * 16, 16), :] = jnp.where(
                inside, cell, 0.0
            ).reshape(8, 16, 128)

    def back(value):
        return jnp.dot(flip_back, value, preferred_element_type=F32).astype(BF)

    sibling_part = right.at[pl.ds(0, 16)]

    def add_from(half, part, total):
        def add(n, total):
            c = (n // 4) * 8 + half * 4 + lax.rem(n, 4)
            a = left[c, pl.ds(part * 32, 32), :].astype(F32).reshape(4, 1, 8, 128)
            b = right[c].astype(F32).reshape(1, 8, 8, 128)
            return total + a * b

        return lax.fori_loop(0, 16, add, total)

    if True:
        @pl.when(core != z_hi)
        def _():
            wait_bytes(sibling_part, r_recv)

        wait_bytes(left.at[pl.ds(0, 15)], l_recv)
        for part in range(4):
            partial[part] = add_from(z_hi, part, jnp.zeros((4, 8, 8, 128), F32))
        wait_bytes(left.at[pl.ds(0, 15)], l_recv2)

        @pl.when(core == z_hi)
        def _():
            wait_bytes(sibling_part, r_recv)

        contact = mask_column(cmask_v[...])
        for half in range(2):
            for part in (2 * half, 2 * half + 1):
                total = add_from(1 - z_hi, part, partial[part])
                sums[pl.ds(part * 32, 32), :] = jnp.sum(total, axis=2).reshape(32, 128)
            rows = slice(64 * half, 64 * half + 64)
            product_norm = layer_norm(sums[rows, :]).astype(BF)
            new = (
                pair[rows]
                + gating[rows] * jnp.dot(product_norm, wout_v[...], preferred_element_type=F32)
            ).astype(BF).astype(F32)
            sums[rows, :] = new
            first[7, rows, :] = (layer_norm(new) * contact[rows]).astype(BF)
            for shift in (-inward, -2 * inward, inward, 2 * inward):
                @pl.when(on_map(col + shift))
                def _():
                    block = pl.ds(64 * half, 64)
                    remote(
                        first.at[7, block], first.at[7 - shift, block], f_send.at[2 + shift],
                        f_recv.at[2 - shift], row, col + shift,
                    ).start()

    if True:
        for shift in SHIFTS:
            @pl.when(jnp.logical_not(on_map(col - shift)))
            def _():
                first[7 - shift] = jnp.zeros((128, 128), BF)

        def hand_rows(delta):
            block = first.at[7 + delta]

            @pl.when(row < ROWS - 1)
            def _():
                remote(
                    block, first.at[2 + delta], f_send2.at[0], f_recv2.at[0, 2 + delta], row + 1, col
                ).start()

            @pl.when(row > 0)
            def _():
                remote(
                    block, first.at[12 + delta], f_send2.at[1], f_recv2.at[1, 2 + delta], row - 1, col
                ).start()

        def take_column(delta):
            @pl.when(on_map(col + delta))
            def _():
                wait_bytes(first.at[7], f_recv.at[2 + delta])

            hand_rows(delta)

        hand_rows(0)
        wait_cols(cots, c_send, c_recv)
        along_rows(cots, c_send2, c_recv2)
        take_column(inward)
        take_column(2 * inward)
        wait_rows(cots, c_send2, c_recv2)
    if True:
        unfold(cots, cfield, range(15))
        shifted(cfield, ctaps, 8, two_rate, 32, -1)
        back_two = jnp.concatenate([two_v[t].T for t in range(9)], axis=0)
        ghid[...] = jnp.dot(
            windows(ctaps, 8, two_rate, 24, -1), back_two, preferred_element_type=F32
        )
    if True:
        take_column(-inward)
        take_column(-2 * inward)
        unfold(first, field, range(5, 10))
    if True:
        for shift in SHIFTS:
            @pl.when(on_map(col + shift))
            def _():
                wait_bytes(first.at[7], f_send.at[2 + shift])

        for delta in range(5):
            @pl.when(row < ROWS - 1)
            def _():
                wait_bytes(first.at[7], f_recv2.at[1, delta])

            @pl.when(row > 0)
            def _():
                wait_bytes(first.at[7], f_recv2.at[0, delta])

        @pl.when(row < ROWS - 1)
        def _():
            wait_bytes(first.at[pl.ds(0, 5)], f_send2.at[0])

        @pl.when(row > 0)
        def _():
            wait_bytes(first.at[pl.ds(0, 5)], f_send2.at[1])

    if True:
        unfold(first, field, [*range(5), *range(10, 15)])
        shifted(field, taps, 8, one_rate, 32, 1)
    if True:
        pre = jnp.dot(
            windows(taps, 8, one_rate, 24, 1), one_v[...].reshape(1152, 128),
            preferred_element_type=F32,
        )
        c_at = lax.broadcasted_iota(jnp.int32, (24, 32, 128), 0) + (col * 8 - 8)
        r_at = lax.broadcasted_iota(jnp.int32, (24, 32, 128), 1) + (row * 16 - 8)
        inside = (c_at >= 0) & (c_at < 256) & (r_at >= 0) & (r_at < 256)
        sigma = jax.nn.sigmoid(pre)
        hidden[...] = jnp.where(inside, (pre * sigma).reshape(24, 32, 128), 0.0)
        gpre[...] = jnp.where(
            inside, (ghid[...] * sigma * (1.0 + pre * (1.0 - sigma))).reshape(24, 32, 128), 0.0
        )
        shifted(hidden, htaps, 8, two_rate, 16, 1)
    over = (((0,), (0,)), ((), ()))

    def scatter(there, chunk):
        def one(k):
            peer = plane_peer(col, k)

            @pl.when((k > 0) | (there != core))
            def _():
                remote(
                    grads.at[there * 16 + plane_slot(peer), CHUNKS[chunk]],
                    parts.at[me, CHUNKS[chunk]], send1, recv1.at[chunk],
                    row - core + there, peer,
                ).start()

        each(0, 16, one)

    def padded(value):
        return jnp.concatenate([value.astype(BF), jnp.zeros((128, 128), BF)]).reshape(16, 80, 128)

    if True:
        cot_own = cots[7]
        second_taps = back(windows(htaps, 8, two_rate, 8, 1))
        grads[pl.ds(16, 16)] = padded(
            lax.dot_general(second_taps, cot_own, over, preferred_element_type=F32)
        )
        scatter(1, 0)
    if True:
        gpre_own = gpre[pl.ds(8, 8), pl.ds(8, 16), :].reshape(128, 128).astype(BF)
        first_taps = windows(taps, 16, one_rate, 8, 1, pl.ds(8, 16))
        grads[pl.ds(0, 16)] = padded(
            lax.dot_general(first_taps, gpre_own, over, preferred_element_type=F32)
        )
        scatter(0, 0)
        scatter(1, 1)
        scatter(0, 1)
    if True:
        parts[me] = grads[me]
        updated = sums[...]
        centre = updated - jnp.mean(updated, axis=-1, keepdims=True)
        inv = lax.rsqrt(jnp.mean(centre * centre, axis=-1, keepdims=True) + EPSILON)
        scaled = centre * inv
        second_pre = jnp.dot(
            second_taps, two_v[...].reshape(1152, 128), preferred_element_type=F32
        )
        output_ref[...] = (updated + second_pre).astype(BF)
        shifted(gpre, gtaps, 8, one_rate, 16, -1)
        back_one = jnp.concatenate([one_v[t].T for t in range(9)], axis=0)
        grad_in = contact * jnp.dot(
            back(windows(gtaps, 8, one_rate, 8, -1)), back_one, preferred_element_type=F32
        )
        grad_norm = inv * (
            grad_in
            - jnp.mean(grad_in, axis=-1, keepdims=True)
            - scaled * jnp.mean(grad_in * scaled, axis=-1, keepdims=True)
        )
        gpair_ref[...] = (cot_own.astype(F32) + grad_norm).astype(BF)

    def added(buf, count, chunk):
        total = buf[0, CHUNKS[chunk], :].astype(F32)
        for n in range(1, count):
            total = total + buf[n, CHUNKS[chunk], :].astype(F32)
        return total.astype(BF)

    most = parts.at[pl.ds(0, 31)]
    three = near.at[pl.ds(0, 3)]
    if True:
        for chunk, rows in enumerate(CHUNKS):
            wait_bytes(parts.at[pl.ds(0, 31), rows], recv1.at[chunk])
            near[near_place, rows, :] = added(parts, 32, chunk)
            block = near.at[near_place, rows]
            for k in range(1, 4):
                remote(block, block, send2, recv2.at[chunk], near_row(k), col).start()
    if True:
        for chunk, rows in enumerate(CHUNKS):
            wait_bytes(near.at[pl.ds(0, 3), rows], recv2.at[chunk])
            apart[far_place, rows, :] = added(near, 4, chunk)
            block_far = apart.at[far_place, rows]
            for k in (2, 1, 3):
                remote(block_far, block_far, send3, recv3.at[chunk], *far_at(k)).start()
    if True:
        for chunk, rows in enumerate(CHUNKS):
            wait_bytes(apart.at[pl.ds(0, 3), rows], recv3.at[chunk])
            final[me, rows, :] = added(apart, 4, chunk)
            whole = final.at[me, rows]
            each(1, 16, lambda k: remote(
                whole, whole, send4, recv4.at[chunk, plane_slot(col)], row, plane_peer(col, k)
            ).start())
            remote(whole, whole, send4, recv5, sibling, col).start()

        for chunk, rows in enumerate(CHUNKS):
            def hand_on(k):
                slot = plane_slot(plane_peer(col, k))
                block = final.at[core * 16 + slot, rows]
                wait_bytes(block, recv4.at[chunk, slot])
                remote(block, block, send4, recv5, sibling, col).start()

            each(1, 16, hand_on)
        wait_bytes(right.at[pl.ds(0, 28)], r_send)
        wait_bytes(left.at[pl.ds(0, 31)], l_send)
        wait_bytes(most, send1)
        wait_bytes(three, send2)
        wait_bytes(three, send3)
        wait_bytes(final.at[pl.ds(0, 16)], recv5)
    if True:
        wait_bytes(most, send4)
        total_ref[...] = final[...]


def finish_kernel(output_in, gpair_in, total_in, output_ref, gpair_ref, one_ref, two_ref):
    output_ref[...] = output_in[...]
    gpair_ref[...] = gpair_in[...]
    for half, ref in enumerate((one_ref, two_ref)):
        grad = total_in[pl.ds(16 * half, 16)].reshape(1280, 128)[:1152].astype(F32)
        ref[...] = (grad * (1.0 / 256.0)).reshape(9, 128, 128)


VMEM = pltpu.VMEM
DMA = pltpu.SemaphoreType.DMA


def shape(dims, dtype):
    return jax.ShapeDtypeStruct(dims, dtype)


def local(
    pair, pair_mask, contact_mask, dilations, w_proj, w_gate, w_out, conv_one, conv_two, cotangent
):
    inputs = (
        pair.reshape(128, 128), pair_mask.T, contact_mask.T, dilations, w_proj, w_gate, w_out,
        conv_one, conv_two, cotangent.reshape(128, 128),
    )
    output, grad_pair, total = pl.pallas_call(
        kernel,
        out_shape=(shape((128, 128), BF), shape((128, 128), BF), shape((32, 80, 128), BF)),
        in_specs=[pl.BlockSpec(memory_space=pltpu.HBM)] * 10,
        out_specs=(pl.BlockSpec(memory_space=pltpu.VMEM),) * 3,
        scratch_shapes=[
            VMEM((128, 128), BF), VMEM((8, 16), jnp.int32), VMEM((8, 16), jnp.int32),
            pltpu.SMEM((2,), jnp.int32), VMEM((128, 512), BF), VMEM((128, 128), BF),
            VMEM((128, 128), BF), VMEM((9, 128, 128), BF), VMEM((9, 128, 128), BF), DMA((10,)),
            VMEM((32, 128, 128), BF), VMEM((32, 64, 128), BF), VMEM((2, 64, 128), BF),
            VMEM((15, 128, 128), BF), VMEM((15, 128, 128), BF), VMEM((128, 128), F32),
            VMEM((40, 48, 128), F32), VMEM((3, 40, 32, 128), BF),
            VMEM((40, 48, 128), F32), VMEM((3, 40, 32, 128), BF),
            VMEM((24, 32, 128), F32), VMEM((3, 24, 16, 128), BF),
            VMEM((24, 32, 128), F32), VMEM((3, 24, 16, 128), BF), VMEM((768, 128), F32),
            VMEM((32, 80, 128), BF), VMEM((32, 80, 128), BF), VMEM((4, 80, 128), BF),
            VMEM((4, 80, 128), BF), VMEM((32, 80, 128), BF), VMEM((4, 4, 8, 8, 128), F32),
            DMA, DMA, DMA, DMA, DMA((4,)), DMA((4,)), DMA, DMA, DMA((4,)),
            DMA((4,)), DMA((4,)), DMA((2,)), DMA((2,)),
            DMA((5,)), DMA((5,)), DMA((2,)), DMA((2, 5)),
            DMA, DMA((2,)), DMA, DMA((2,)), DMA, DMA((2,)), DMA, DMA((2, 16)), DMA,
        ],
        compiler_params=pltpu.CompilerParams(
            collective_id=1, has_side_effects=True, vmem_limit_bytes=62 << 20
        ),
    )(*inputs)
    whole = pl.BlockSpec(memory_space=pltpu.VMEM)
    output, grad_pair, grad_one, grad_two = pl.pallas_call(
        finish_kernel,
        out_shape=(
            shape((128, 128), BF), shape((128, 128), BF),
            shape((9, 128, 128), F32), shape((9, 128, 128), F32),
        ),
        in_specs=[whole] * 3,
        out_specs=(whole,) * 4,
    )(output, grad_pair, total)
    return (output.reshape(16, 8, 128), grad_pair.reshape(16, 8, 128), grad_one, grad_two)


def solution(mesh):
    in_specs = (
        P("row", "col", None), P("row", "col"), P("row", "col"), P(), P(), P(), P(), P(), P(),
        P("row", "col", None),
    )
    out_specs = (P("row", "col", None), P("row", "col", None), P(), P())
    return jax.shard_map(local, mesh=mesh, in_specs=in_specs, out_specs=out_specs, check_vma=False)
```
